256 devices in a mesh: branch: 2 (over core), seq: 16 (over x, z_lo), head: 8 (over y, z_hi).
Axes of the slice: x: 4, y: 4, z: 8 (z_hi: 2, z_lo: 4; z = z_hi * 4 + z_lo), core: 2. Of those that a mesh axis runs over, the one named last changes fastest.
Arguments:
- latent: float32 [8192, 3072], P(('seq', 'head')), may hold values from -8 to 8
- modulation: float32 [2, 3, 3072], P('branch'), may hold values from -1.2 to 1.2
- w_qkv: bfloat16 [3072, 24, 384], P(None, 'head'), may hold values from -5 to 5
- w_out: bfloat16 [24, 128, 3072], P('head'), may hold values from -0.5 to 0.5
- timestep: int32 [1], replicated, may hold values from 0 to 49
Outputs:
- stepped: float32 [8192, 3072], P(('seq', 'head'))
- denoised: float32 [8192, 3072], P(('seq', 'head'))
The draws below stay inside these ranges and needn't reach their ends.
Inputs may be any that keep to these rules, and one draw needn't show every extreme that they name: `timestep`: one step index of the plan of 50 steps.
All inputs are finite; a program needn't handle non-finite values.
Results may differ from the reference program's by a relative error of at most 0.0055.
Values may be sent and summed in bfloat16 or wider, within the bound.
A program may use at most 128 MiB of HBM per device.

```python
import math
import jax
import jax.numpy as jnp
from jax import lax

D = 3072
HEADS = 24
DH = 128
STEPS = 50
SEQ = 8192
N_BRANCH = 2


def draw_latent(key, part):
    key = jax.random.fold_in(key, 11)
    key_base = jax.random.fold_in(key, 0)
    return jnp.clip(jax.random.normal(key_base, (SEQ, D)), -6.0, 6.0)


def draw_w_qkv(key, part):
    key = jax.random.fold_in(key, 23)
    key_main = jax.random.fold_in(key, 0)
    spread_std = D ** (-0.5)
    return (jnp.clip(jax.random.normal(key_main, (D, HEADS, 3 * DH)), -4.0, 4.0) * spread_std).astype(jnp.bfloat16)


def levels(stream_key, extent, cuts, smallest, largest):
    factor_of, own = 1.0, jax.random.fold_in(stream_key, 6)
    for axis_at, shards_of in cuts:
        draws = jnp.exp(jax.random.uniform(jax.random.fold_in(own, axis_at), (shards_of,), jnp.float32, smallest / len(cuts), largest / len(cuts)))
        factor_of = factor_of * jnp.repeat(draws, extent[axis_at] // shards_of).reshape([-1 if axis == axis_at else 1 for axis in range(len(extent))])
    return factor_of


def gaussian(rng, extent, spread, reach, cuts=(), held_as=jnp.bfloat16):
    drawn = jax.random.normal(rng, extent, jnp.float32) * spread
    if len(cuts) > 0:
        drawn = levels(rng, extent, cuts, -0.22, 0.18) * drawn
    return jnp.clip(drawn, min=-reach, max=reach).astype(held_as)


def setup_inputs(seed: int = 0) -> dict:
    arg_keys = jax.random.split(jax.random.key(seed), 6)
    return {
        "latent": draw_latent(jax.random.fold_in(arg_keys[5], 71), 0),
        "modulation": gaussian(arg_keys[1], (N_BRANCH, 3, D), 0.3, 1.2, ((0, 2),), jnp.float32),
        "w_qkv": draw_w_qkv(jax.random.fold_in(arg_keys[5], 71), 0),
        "w_out": gaussian(arg_keys[3], (HEADS, DH, D), DH ** -0.5, 0.5, ((0, 8),)),
        "timestep": jax.random.randint(arg_keys[4], (1,), 0, STEPS).astype(jnp.int32),
    }


guidance_scale = 6.0
flow_shift = 7.0
epsilon = 1e-06

def sigma_at(step_value):
    fraction = 1.0 - step_value / STEPS
    return flow_shift * fraction / (1.0 + (flow_shift - 1.0) * fraction)

def modulate(latent, shift_vec, scale_vec):
    row_mean = lax.optimization_barrier(jnp.mean(latent, axis=1, keepdims=True))
    centred = latent - row_mean
    row_var = lax.optimization_barrier(jnp.mean(centred * centred, axis=1, keepdims=True))
    return (centred * lax.rsqrt(row_var + epsilon) * (1.0 + scale_vec) + shift_vec).astype(jnp.bfloat16)

def attend(query_rows, key_rows, value_rows):
    total_len = query_rows.shape[1]
    block_len = math.gcd(total_len, 512)
    score_scale = DH ** (-0.5)

    def per_head(head_parts):
        q_head, k_head, v_head = head_parts

        def per_block(q_block):
            scores = jnp.dot(q_block, k_head.T, preferred_element_type=jnp.float32) * score_scale
            peak = lax.optimization_barrier(jnp.max(scores, axis=1, keepdims=True))
            expo = jnp.exp(scores - peak)
            totals = lax.optimization_barrier(jnp.sum(expo, axis=1, keepdims=True))
            mixed_out = jnp.dot(expo.astype(jnp.bfloat16), v_head, preferred_element_type=jnp.float32)
            return (mixed_out / totals).astype(jnp.bfloat16)
        blocks = lax.map(per_block, q_head.reshape(total_len // block_len, block_len, DH))
        return blocks.reshape(total_len, DH)
    return lax.map(per_head, (query_rows, key_rows, value_rows))

def reference(latent, modulation, w_qkv, w_out, timestep):
    velocity = latent
    flat_in = w_qkv.reshape(w_qkv.shape[0], HEADS * 3 * DH)
    flat_out = w_out.reshape(HEADS * DH, w_out.shape[2])
    for branch in range(2):
        branch_weight = guidance_scale if branch == 0 else 1.0 - guidance_scale
        normed = modulate(latent, modulation[branch, 0], modulation[branch, 1])
        qkv_all = jnp.dot(normed, flat_in, preferred_element_type=jnp.float32).astype(jnp.bfloat16)
        qkv_all = qkv_all.reshape(SEQ, HEADS, 3 * DH)
        query_rows = jnp.transpose(qkv_all[:, :, :DH], (1, 0, 2))
        key_rows = jnp.transpose(qkv_all[:, :, DH:2 * DH], (1, 0, 2))
        value_rows = jnp.transpose(qkv_all[:, :, 2 * DH:], (1, 0, 2))
        attended = attend(query_rows, key_rows, value_rows)
        merged = jnp.transpose(attended, (1, 0, 2)).reshape(SEQ, HEADS * DH)
        projected = jnp.dot(merged, flat_out, preferred_element_type=jnp.float32)
        velocity = velocity + branch_weight * modulation[branch, 2] * projected
    moment = timestep[0].astype(jnp.float32)
    sigma_now = sigma_at(moment)
    step_size = sigma_at(moment + 1.0) - sigma_now
    return (latent + step_size * velocity, latent - sigma_now * velocity)
```

```python
import functools

import jax
import jax.numpy as jnp
from jax import lax
from jax.experimental import pallas as pl
from jax.experimental.pallas import tpu as pltpu
from jax.sharding import PartitionSpec as P

STEPS = 50
GUIDANCE = 6.0
SHIFT = 7.0
EPS = 1e-06
LOG2E = 1.4426950408889634
MESH = pl.DeviceIdType.MESH
F32, BF16 = jnp.float32, jnp.bfloat16

D = 3072
DH = 128
H = 3
NX, NY, NZ = 4, 4, 4
ROWS = 32
HALF = 2 * NY * ROWS
YD = (1, 3, 2)
XD = (1, 3, 2)
ZD = (2, 3, 1)


def sigma_at(step_value):
    fraction = 1.0 - step_value / STEPS
    return SHIFT * fraction / (1.0 + (SHIFT - 1.0) * fraction)


def toggled(z, k):
    if k == 1:
        return z + 1 - 2 * (z % 2)
    if k == 2:
        return z + 2 - 4 * (z // 2)
    return 3 - z


def kernel(
    lat_ref, mod_ref, wq_hbm, wo_hbm, out_ref,
    wq, wo, xh, nm, qb, kb, vb, osend, orecv, lsend, lrecv, att, attx, gate, gatex,
    psend, precv, zsend, zrecv, fin, finx,
    w_sem, xs_sem, xr_sem, g_sem, qs_sem, qr_sem, ks_sem, kr_sem, vs_sem, vr_sem,
    os_sem, or_sem, ls_sem, lr_sem, as_sem, ar_sem, ps_sem, pr_sem, e_sem,
):
    b, s, h = lax.axis_index("branch"), lax.axis_index("seq"), lax.axis_index("head")
    x, z, y, zh = s // NZ, s % NZ, h // 2, h % 2

    def to_y(d):
        return (b, s, ((y + d) % NY) * 2 + zh)

    def to_x(d):
        return (b, ((x + d) % NX) * NZ + z, h)

    def to_z(k):
        return (b, x * NZ + toggled(z, k), h)

    far = (b, s, h + 1 - 2 * zh)
    twin = (1 - b, s, h)

    def remote(src, dst, ssem, rsem, dev):
        return pltpu.make_async_remote_copy(
            src_ref=src, dst_ref=dst, send_sem=ssem, recv_sem=rsem,
            device_id=dev, device_id_type=MESH,
        )

    load_q = pltpu.make_async_copy(wq_hbm, wq, w_sem.at[0])
    load_o = pltpu.make_async_copy(wo_hbm, wo, w_sem.at[1])
    load_q.start()
    load_o.start()

    barrier = pltpu.get_barrier_semaphore()
    peers = [to_y(d) for d in YD] + [to_x(d) for d in XD] + [to_z(k) for k in ZD] + [far, twin]
    for dev in peers:
        pl.semaphore_signal(barrier, inc=1, device_id=dev, device_id_type=MESH)

    def normalise(at):
        rows = lat_ref[pl.ds(pl.multiple_of(at * ROWS, ROWS), ROWS), :]
        centred = rows - jnp.mean(rows, axis=1, keepdims=True)
        var = jnp.mean(centred * centred, axis=1, keepdims=True)
        return (centred * lax.rsqrt(var + EPS)).astype(BF16)

    xh[0, 0, 0] = normalise(b)
    weight = jnp.where(b == 0, GUIDANCE, 1.0 - GUIDANCE).astype(F32)
    gate[...] = jnp.broadcast_to(weight * mod_ref[2:3, :], gate.shape)
    pl.semaphore_wait(barrier, len(peers))

    sends = []

    def go(copy):
        copy.start()
        sends.append(copy)
        return copy

    def x_copy(src, dst, dev):
        return remote(xh.at[src], xh.at[dst], xs_sem.at[dst], xr_sem.at[dst], dev)

    own = (0, 0, 0)
    from_far = go(x_copy(own, (1, 0, 0), far))
    from_y = [go(x_copy(own, (0, 0, d), to_y(d))) for d in YD]
    from_twin0, from_twin1 = [], []
    gate_copy = go(remote(gate, gatex, g_sem.at[0], g_sem.at[1], twin))
    xh[0, 1, 0] = normalise(1 - b)
    for d, copy in zip(YD, from_y):
        copy.wait_recv()
        from_twin0.append(go(x_copy((0, 0, d), (0, 1, d), twin)))
    from_far.wait_recv()
    from_y = [go(x_copy((1, 0, 0), (1, 0, d), to_y(d))) for d in YD]
    from_twin1.append(go(x_copy((1, 0, 0), (1, 1, 0), twin)))

    shift, scale = mod_ref[0:1, :], 1.0 + mod_ref[1:2, :]
    q_scale = DH**-0.5 * LOG2E
    q_in, kv_in = {}, {}

    def project(dz):
        for half in range(2):
            for dy in range(NY):
                nm[pl.ds((half * NY + dy) * ROWS, ROWS), :] = (
                    xh[dz, half, dy].astype(F32) * scale + shift
                ).astype(BF16)

        def per_head(i, carry):
            got = jnp.dot(nm[...], wq[i], preferred_element_type=F32)
            qb[0, dz, i] = (got[:, :DH] * q_scale).astype(BF16)
            kb[0, dz, i] = got[:, DH : 2 * DH].T.astype(BF16)
            vb[0, dz, i] = got[:, 2 * DH :].astype(BF16)
            return carry

        lax.fori_loop(0, H, per_head, 0)
        for d in XD:
            kv_in[d, dz, 0] = go(remote(kb.at[0, dz], kb.at[d, dz], ks_sem.at[d, dz], kr_sem.at[d, dz], to_x(d)))
            kv_in[d, dz, 1] = go(remote(vb.at[0, dz], vb.at[d, dz], vs_sem.at[d, dz], vr_sem.at[d, dz], to_x(d)))
        for k in ZD:
            q_in[k, dz] = go(remote(qb.at[0, dz], qb.at[k, dz], qs_sem.at[k, dz], qr_sem.at[k, dz], to_z(k)))

    for copy in from_twin0:
        copy.wait_recv()
    load_q.wait()
    project(0)
    for d, copy in zip(YD, from_y):
        copy.wait_recv()
        from_twin1.append(go(x_copy((1, 0, d), (1, 1, d), twin)))
    for copy in from_twin1:
        copy.wait_recv()
    project(1)

    for copy in kv_in.values():
        copy.wait_recv()

    lane = lax.broadcasted_iota(jnp.int32, (HALF, DH), 1)

    def attend(k, dz):
        packed = jnp.zeros((HALF, DH), F32)
        for i in range(H):
            query = qb[k, dz, i]
            scores = jnp.concatenate(
                [
                    jnp.dot(query, kb[d, e, i], preferred_element_type=F32)
                    for d in range(NX)
                    for e in range(2)
                ],
                axis=1,
            )
            peak = jnp.max(scores, axis=1, keepdims=True)
            expo = jnp.exp2(scores - peak)
            total = jnp.sum(expo, axis=1, keepdims=True)
            probs = expo.astype(BF16)
            mixed = jnp.zeros((HALF, DH), F32)
            for d in range(NX):
                for e in range(2):
                    at = (d * 2 + e) * HALF
                    mixed += jnp.dot(probs[:, at : at + HALF], vb[d, e, i], preferred_element_type=F32)
            osend[k, dz, i] = (mixed / total).astype(BF16)
            packed = jnp.where(lane == i, peak + jnp.log2(total), packed)
        lsend[k, dz] = packed.T[:8, :]

    o_in, l_in = {}, {}
    for k in ZD + (0,):
        if k:
            for dz in range(2):
                q_in[k, dz].wait_recv()

        def per_dz(i, carry, k=k):
            attend(k, 1 - i)
            return carry

        lax.fori_loop(0, 2, per_dz, 0)
        if k:
            for dz in (1, 0):
                o_in[k, dz] = go(remote(osend.at[k, dz], orecv.at[k, dz], os_sem.at[k, dz], or_sem.at[k, dz], to_z(k)))
                l_in[k, dz] = go(remote(lsend.at[k, dz], lrecv.at[k, dz], ls_sem.at[k, dz], lr_sem.at[k, dz], to_z(k)))

    load_o.wait()
    gate_copy.wait_recv()

    def merge(dz):
        logs = [
            jnp.concatenate([ref, jnp.zeros((DH - 8, HALF), F32)], axis=0).T
            for ref in [lsend[0, dz]] + [lrecv[k, dz] for k in ZD]
        ]
        peak = functools.reduce(jnp.maximum, logs)
        parts = [jnp.exp2(log - peak) for log in logs]
        total = functools.reduce(jnp.add, parts)
        for i in range(H):
            mixed = jnp.zeros((HALF, DH), F32)
            for part, ref in zip(parts, [osend.at[0]] + [orecv.at[k] for k in ZD]):
                mixed += (part / total)[:, i : i + 1] * ref[dz, i].astype(F32)
            mixed = mixed.astype(BF16)
            att[dz, 0, :, i * DH : (i + 1) * DH] = mixed[: HALF // 2]
            att[dz, 1, :, i * DH : (i + 1) * DH] = mixed[HALF // 2 :]
        return go(remote(att.at[dz, 1], attx.at[dz], as_sem.at[dz], ar_sem.at[dz], twin))

    a_in = {}
    for dz in (1, 0):
        for k in ZD:
            o_in[k, dz].wait_recv()
            l_in[k, dz].wait_recv()
        a_in[dz] = merge(dz)

    p_in = {}
    wide = 512
    for dz in (1, 0):
        a_in[dz].wait_recv()

        def per_tile(t, carry, dz=dz):
            cols = pl.ds(pl.multiple_of(t * wide, wide), wide)
            tile = gate[0:1, cols] * jnp.dot(att[dz, 0], wo[:, cols], preferred_element_type=F32)
            tile += gatex[0:1, cols] * jnp.dot(attx[dz], wo[:, cols], preferred_element_type=F32)
            psend[dz, :, :, cols] = tile.astype(BF16).reshape(NY, ROWS, wide)
            return carry

        lax.fori_loop(0, D // wide, per_tile, 0)
        for d in YD:
            p_in[dz, d] = go(remote(psend.at[dz, d], precv.at[dz, d], ps_sem.at[dz, d], pr_sem.at[dz, d], to_y(NY - d)))

    def summed(dz):
        total = psend[dz, 0].astype(F32)
        for d in YD:
            p_in[dz, d].wait_recv()
            total += precv[dz, d].astype(F32)
        return total

    zsend[...] = summed(1).astype(BF16)
    z_copy = go(remote(zsend, zrecv, e_sem.at[0], e_sem.at[1], far))
    fin[...] = summed(0)
    z_copy.wait_recv()
    fin[...] += zrecv[...].astype(F32)
    f_copy = go(remote(fin, finx, e_sem.at[2], e_sem.at[3], twin))
    out_ref[pl.ds(pl.multiple_of(b * ROWS, ROWS), ROWS), :] = fin[...]
    f_copy.wait_recv()
    out_ref[pl.ds(pl.multiple_of((1 - b) * ROWS, ROWS), ROWS), :] = finx[...]

    for copy in sends:
        copy.wait_send()


def guided(latent, modulation, wq, wo):
    dma = pltpu.SemaphoreType.DMA
    vmem = pltpu.VMEM
    scratch = [
        vmem((H, D, 3 * DH), BF16),
        vmem((H * DH, D), BF16),
        vmem((2, 2, NY, ROWS, D), BF16),
        vmem((HALF, D), BF16),
        vmem((NZ, 2, H, HALF, DH), BF16),
        vmem((NX, 2, H, DH, HALF), BF16),
        vmem((NX, 2, H, HALF, DH), BF16),
        vmem((NZ, 2, H, HALF, DH), BF16),
        vmem((NZ, 2, H, HALF, DH), BF16),
        vmem((NZ, 2, 8, HALF), F32),
        vmem((NZ, 2, 8, HALF), F32),
        vmem((2, 2, HALF // 2, H * DH), BF16),
        vmem((2, HALF // 2, H * DH), BF16),
        vmem((8, D), F32),
        vmem((8, D), F32),
        vmem((2, NY, ROWS, D), BF16),
        vmem((2, NY, ROWS, D), BF16),
        vmem((ROWS, D), BF16),
        vmem((ROWS, D), BF16),
        vmem((ROWS, D), F32),
        vmem((ROWS, D), F32),
        dma((2,)),
        dma((2, 2, NY)), dma((2, 2, NY)),
        dma((2,)),
        dma((NZ, 2)), dma((NZ, 2)),
        dma((NX, 2)), dma((NX, 2)),
        dma((NX, 2)), dma((NX, 2)),
        dma((NZ, 2)), dma((NZ, 2)),
        dma((NZ, 2)), dma((NZ, 2)),
        dma((2,)), dma((2,)),
        dma((2, NY)), dma((2, NY)),
        dma((4,)),
    ]
    held = pl.BlockSpec(memory_space=pltpu.VMEM)
    left = pl.BlockSpec(memory_space=pl.ANY)
    return pl.pallas_call(
        kernel,
        out_shape=jax.ShapeDtypeStruct(latent.shape, F32),
        in_specs=[held, held, left, left],
        out_specs=held,
        scratch_shapes=scratch,
        compiler_params=pltpu.CompilerParams(
            collective_id=0, has_side_effects=True, vmem_limit_bytes=60 * 1024 * 1024
        ),
    )(latent, modulation, wq, wo)


def shards(latent, modulation, w_qkv, w_out, timestep):
    wq = jnp.transpose(w_qkv, (1, 0, 2))
    wo = w_out.reshape(H * DH, D)
    change = guided(latent, modulation.reshape(3, D), wq, wo)
    moment = timestep[0].astype(F32)
    sigma_now = sigma_at(moment)
    step_size = sigma_at(moment + 1.0) - sigma_now
    velocity = latent + change
    return (latent + step_size * velocity, latent - sigma_now * velocity)


def solution(mesh):
    placed = (
        P(("seq", "head"), None),
        P("branch", None, None),
        P(None, "head", None),
        P("head", None, None),
        P(),
    )
    return jax.shard_map(
        shards,
        mesh=mesh,
        in_specs=placed,
        out_specs=(P(("seq", "head"), None), P(("seq", "head"), None)),
        check_vma=False,
    )
```

```python
import functools

import jax
import jax.numpy as jnp
from jax import lax
from jax.experimental import pallas as pl
from jax.experimental.pallas import tpu as pltpu
from jax.sharding import PartitionSpec as P

STEPS = 50
GUIDANCE = 6.0
SHIFT = 7.0
EPS = 1e-06
LOG2E = 1.4426950408889634
MESH = pl.DeviceIdType.MESH
F32, BF16 = jnp.float32, jnp.bfloat16

D = 3072
DH = 128
H = 3
NX, NY, NZ = 4, 4, 4
ROWS = 32
HALF = 2 * NY * ROWS
YD = (1, 3, 2)
XD = (1, 3, 2)
ZD = (2, 3, 1)


def sigma_at(step_value):
    fraction = 1.0 - step_value / STEPS
    return SHIFT * fraction / (1.0 + (SHIFT - 1.0) * fraction)


def toggled(z, k):
    if k == 1:
        return z + 1 - 2 * (z % 2)
    if k == 2:
        return z + 2 - 4 * (z // 2)
    return 3 - z


def kernel(
    lat_ref, mod_ref, wq_hbm, wo_hbm, out_ref,
    wq, wo, xh, nm, qb, kv, osend, orecv, lsend, lrecv, att, attx, gate, gatex,
    psend, precv, zsend, zrecv, fin, finx,
    w_sem, xs_sem, xr_sem, g_sem, qs_sem, qr_sem, q3_sem, ks_sem, kr_sem, k2_sem,
    os_sem, or_sem, ls_sem, lr_sem, as_sem, ar_sem, ps_sem, pr_sem, zs_sem, zr_sem, fs_sem, fr_sem,
):
    b, s, h = lax.axis_index("branch"), lax.axis_index("seq"), lax.axis_index("head")
    x, z, y, zh = s // NZ, s % NZ, h // 2, h % 2

    def to_y(d):
        return (b, s, ((y + d) % NY) * 2 + zh)

    def to_x(d):
        return (b, ((x + d) % NX) * NZ + z, h)

    def to_z(k):
        return (b, x * NZ + toggled(z, k), h)

    far = (b, s, h + 1 - 2 * zh)
    twin = (1 - b, s, h)
    inner = (z == 1) | (z == 2)

    def remote(src, dst, ssem, rsem, dev):
        return pltpu.make_async_remote_copy(
            src_ref=src, dst_ref=dst, send_sem=ssem, recv_sem=rsem,
            device_id=dev, device_id_type=MESH,
        )

    load_q = pltpu.make_async_copy(wq_hbm, wq, w_sem.at[0])
    load_o = pltpu.make_async_copy(wo_hbm, wo, w_sem.at[1])
    load_q.start()
    load_o.start()

    barrier = pltpu.get_barrier_semaphore()
    peers = [to_y(d) for d in YD] + [to_x(d) for d in XD] + [to_z(k) for k in ZD] + [far, twin]
    for dev in peers:
        pl.semaphore_signal(barrier, inc=1, device_id=dev, device_id_type=MESH)

    def normalise(at):
        rows = lat_ref[pl.ds(pl.multiple_of(at * ROWS, ROWS), ROWS), :]
        centred = rows - jnp.mean(rows, axis=1, keepdims=True)
        var = jnp.mean(centred * centred, axis=1, keepdims=True)
        return (centred * lax.rsqrt(var + EPS)).astype(BF16).reshape(2, ROWS // 2, D)

    xh[0, 0, 0] = normalise(b)
    weight = jnp.where(b == 0, GUIDANCE, 1.0 - GUIDANCE).astype(F32)
    gate[...] = jnp.broadcast_to(weight * mod_ref[2], gate.shape)
    pl.semaphore_wait(barrier, len(peers))

    sends = []

    def go(copy):
        copy.start()
        sends.append(copy)
        return copy

    def x_copy(src, dst, dev):
        return go(remote(xh.at[src], xh.at[dst], xs_sem.at[dst], xr_sem.at[dst], dev))

    x_in = {}

    def spread(dz, c):
        for d in (1, 3):
            x_in[dz, 0, d, c] = x_copy((dz, 0, 0, c), (dz, 0, d, c), to_y(d))

    def pass_on(dz, d, c):
        x_in[dz, 0, d, c].wait_recv()
        if (d, c) in ((1, 0), (3, 1)):
            x_in[dz, 0, 2, c] = x_copy((dz, 0, d, c), (dz, 0, 2, c), to_y(d))
        x_in[dz, 1, d, c] = x_copy((dz, 0, d, c), (dz, 1, d, c), twin)

    for c in range(2):
        x_in[1, 0, 0, c] = x_copy((0, 0, 0, c), (1, 0, 0, c), far)
        spread(0, c)
    gate_copy = go(remote(gate, gatex, g_sem.at[0], g_sem.at[1], twin))
    xh[0, 1, 0] = normalise(1 - b)

    pass_on(0, 1, 0)
    pass_on(0, 3, 0)
    x_in[1, 0, 0, 0].wait_recv()
    spread(1, 0)
    x_in[1, 1, 0, 0] = x_copy((1, 0, 0, 0), (1, 1, 0, 0), twin)
    pass_on(0, 3, 1)
    pass_on(0, 1, 1)
    x_in[1, 0, 0, 1].wait_recv()
    spread(1, 1)
    x_in[1, 1, 0, 1] = x_copy((1, 0, 0, 1), (1, 1, 0, 1), twin)
    pass_on(0, 2, 0)
    pass_on(0, 2, 1)

    q_scale = DH**-0.5 * LOG2E
    q_in, kv_in = {}, {}

    def project(dz):
        for half in range(2):
            for dy in range(NY):
                if (half, dy) == (1, 0) and dz == 0:
                    continue
                if half == 1:
                    for c in range(2):
                        x_in[dz, 1, dy, c].wait_recv()
        for half in range(2):
            for dy in range(NY):
                nm[pl.ds((half * NY + dy) * ROWS, ROWS), :] = (
                    xh[dz, half, dy].reshape(ROWS, D).astype(F32) * (1.0 + mod_ref[1]) + mod_ref[0]
                ).astype(BF16)
        for i in range(H):
            got = jnp.dot(nm[...], wq[i], preferred_element_type=F32)
            qb[0, i, dz] = (got[:, :DH] * q_scale).astype(BF16)
            for j in range(2):
                rows = slice(j * DH, (j + 1) * DH)
                kv[0, i, dz, j] = got[rows, DH : 2 * DH].T.astype(BF16)
                kv[0, i, dz, 2 + j] = got[rows, 2 * DH :].astype(BF16)
            for d in (1, 3):
                at = (d, i, dz)
                kv_in[at] = go(remote(kv.at[0, i, dz], kv.at[at], ks_sem.at[at], kr_sem.at[at], to_x(d)))
            for k in (2, 1):
                q_in[k, i, dz] = go(
                    remote(qb.at[0, i, dz], qb.at[k, i, dz], qs_sem.at[k, i, dz], qr_sem.at[k, i, dz], to_z(k))
                )
            near = remote(qb.at[0, i, dz], qb.at[3, i, dz], qs_sem.at[3, i, dz], qr_sem.at[3, i, dz], to_z(3))
            q_in[3, i, dz] = near
            pl.when(inner)(near.start)

    def relay_x(dz, i):
        for d, first in ((1, 0), (3, 2)):
            kv_in[d, i, dz].wait_recv()
            half = pl.ds(first, 2)
            kv_in[2, i, dz, first] = go(
                remote(
                    kv.at[d, i, dz, half],
                    kv.at[2, i, dz, half],
                    k2_sem.at[0, i, dz, first // 2],
                    k2_sem.at[1, i, dz, first // 2],
                    to_x(d),
                )
            )

    relays = []

    def relay_z(dz, i):
        q_in[2, i, dz].wait_recv()
        relay = remote(qb.at[2, i, dz], qb.at[3, i, dz], q3_sem.at[i, dz], qr_sem.at[3, i, dz], to_z(1))
        pl.when(inner)(relay.start)
        relays.append(relay)

    load_q.wait()
    project(0)
    pass_on(1, 1, 0)
    pass_on(1, 3, 0)
    relay_x(0, 0)
    pass_on(1, 3, 1)
    pass_on(1, 1, 1)
    relay_x(0, 1)
    relay_z(0, 0)
    pass_on(1, 2, 0)
    pass_on(1, 2, 1)
    relay_x(0, 2)
    relay_z(0, 1)
    project(1)
    relay_z(0, 2)
    for i in range(H):
        relay_x(1, i)
        relay_z(1, i)

    def attend(k, i, e):
        query = qb[k, i, e]
        scores = jnp.concatenate(
            [
                jnp.dot(
                    query,
                    jnp.concatenate([kv[d, i, f, 0], kv[d, i, f, 1]], axis=1),
                    preferred_element_type=F32,
                )
                for d in range(NX)
                for f in range(2)
            ],
            axis=1,
        )
        peak = jnp.max(scores, axis=1, keepdims=True)
        expo = jnp.exp2(scores - peak)
        total = jnp.sum(expo, axis=1, keepdims=True)
        probs = expo.astype(BF16)
        mixed = jnp.zeros((HALF, DH), F32)
        for d in range(NX):
            for f in range(2):
                at = (d * 2 + f) * HALF
                mixed += jnp.dot(
                    probs[:, at : at + HALF], kv[d, i, f, 2:4].reshape(HALF, DH), preferred_element_type=F32
                )
        osend[k, i, e] = (mixed / total).astype(BF16)
        lsend[k, i, e] = jnp.broadcast_to(peak + jnp.log2(total), (HALF, DH)).T[:8, :]

    o_in = {}

    def send_back(k, i, e, slot, dev):
        at = (slot, i, e)
        o_in[at] = [
            go(remote(osend.at[k, i, e], orecv.at[at], os_sem.at[at], or_sem.at[at], dev)),
            go(remote(lsend.at[k, i, e], lrecv.at[at], ls_sem.at[at], lr_sem.at[at], dev)),
        ]

    def merged(parts):
        logs = [log[...] for _, log in parts]
        peak = functools.reduce(jnp.maximum, logs)
        shares = [jnp.exp2(log - peak) for log in logs]
        total = functools.reduce(jnp.add, shares)
        mixed = jnp.zeros((HALF, DH), F32)
        for share, (out, _) in zip(shares, parts):
            spread_out = jnp.concatenate([share / total] * (DH // 8), axis=0).T
            mixed += spread_out * out[...].astype(F32)
        return mixed.astype(BF16), peak + jnp.log2(total)

    def cross(i, e):
        for copy in o_in[3, i, e]:
            copy.wait_recv()
        out, log = merged(
            [(osend.at[2, i, e], lsend.at[2, i, e]), (orecv.at[3, i, e], lrecv.at[3, i, e])]
        )
        osend[4, i, e] = out
        lsend[4, i, e] = log
        send_back(4, i, e, 2, to_z(2))

    def merge(i, e):
        for k in (1, 2):
            for copy in o_in[k, i, e]:
                copy.wait_recv()
        out, _ = merged(
            [(osend.at[0, i, e], lsend.at[0, i, e])]
            + [(orecv.at[k, i, e], lrecv.at[k, i, e]) for k in (1, 2)]
        )
        att[e, 0, :, i * DH : (i + 1) * DH] = out[: HALF // 2]
        att[e, 1, :, i * DH : (i + 1) * DH] = out[HALF // 2 :]

    def outgoing(i, e):
        for k in (3, 1):
            q_in[k, i, e].wait_recv()
            attend(k, i, e)
            send_back(k, i, e, k, to_z(1))

    def staying(i, e):
        attend(2, i, e)
        attend(0, i, e)

    a_in, p_in = {}, {}
    wide = D // 2
    tile = 512

    def exchange(dz):
        for i in range(H):
            merge(i, dz)
        a_in[dz] = go(remote(att.at[dz, 1], attx.at[dz], as_sem.at[dz], ar_sem.at[dz], twin))

    def project_out(dz):
        a_in[dz].wait_recv()
        for c in range(2):
            for t in range(wide // tile):
                cols = slice(c * wide + t * tile, c * wide + (t + 1) * tile)
                part = gate[0:1, cols] * jnp.dot(att[dz, 0], wo[:, cols], preferred_element_type=F32)
                part += gatex[0:1, cols] * jnp.dot(attx[dz], wo[:, cols], preferred_element_type=F32)
                psend[dz, c, :, :, t * tile : (t + 1) * tile] = part.astype(BF16).reshape(NY, ROWS, tile)
            for d in (2, 1, 3):
                at = (dz, c, d)
                p_in[at] = go(remote(psend.at[at], precv.at[at], ps_sem.at[at], pr_sem.at[at], to_y(NY - d)))

    before = None
    for e in (1, 0):
        for i in range(H):
            if e == 1:
                for dz in range(2):
                    for first in (0, 2):
                        kv_in[2, i, dz, first].wait_recv()
            outgoing(i, e)
            if before:
                cross(*before)
            before = (i, e)
            if (i, e) == (2, 0):
                project_out(1)
            staying(i, e)
            if (i, e) == (1, 0):
                load_o.wait()
                gate_copy.wait_recv()
                exchange(1)
    cross(*before)

    def summed(dz, c):
        total = psend[dz, c, 0].astype(F32)
        for d in YD:
            p_in[dz, c, d].wait_recv()
            total += precv[dz, c, d].astype(F32)
        return total

    z_in, f_in = [], []
    for c in range(2):
        zsend[c] = summed(1, c).astype(BF16)
        z_in.append(go(remote(zsend.at[c], zrecv.at[c], zs_sem.at[c], zr_sem.at[c], far)))
    exchange(0)
    project_out(0)
    for c in range(2):
        whole = summed(0, c)
        z_in[c].wait_recv()
        whole += zrecv[c].astype(F32)
        fin[c] = whole
        f_in.append(go(remote(fin.at[c], finx.at[c], fs_sem.at[c], fr_sem.at[c], twin)))
        out_ref[pl.ds(pl.multiple_of(b * ROWS, ROWS), ROWS), c * wide : (c + 1) * wide] = whole
    for c in range(2):
        f_in[c].wait_recv()
        out_ref[pl.ds(pl.multiple_of((1 - b) * ROWS, ROWS), ROWS), c * wide : (c + 1) * wide] = finx[c]

    for copy in sends:
        copy.wait_send()

    @pl.when(inner)
    def _():
        for copy in relays:
            copy.wait_send()
        for i in range(H):
            for dz in range(2):
                q_in[3, i, dz].wait_send()


def guided(latent, modulation, wq, wo):
    dma = pltpu.SemaphoreType.DMA
    vmem = pltpu.VMEM
    scratch = [
        vmem((H, D, 3 * DH), BF16),
        vmem((H * DH, D), BF16),
        vmem((2, 2, NY, 2, ROWS // 2, D), BF16),
        vmem((HALF, D), BF16),
        vmem((NZ, H, 2, HALF, DH), BF16),
        vmem((NX, H, 2, 4, DH, DH), BF16),
        vmem((NZ + 1, H, 2, HALF, DH), BF16),
        vmem((NZ, H, 2, HALF, DH), BF16),
        vmem((NZ + 1, H, 2, 8, HALF), F32),
        vmem((NZ, H, 2, 8, HALF), F32),
        vmem((2, 2, HALF // 2, H * DH), BF16),
        vmem((2, HALF // 2, H * DH), BF16),
        vmem((8, D), F32),
        vmem((8, D), F32),
        vmem((2, 2, NY, ROWS, D // 2), BF16),
        vmem((2, 2, NY, ROWS, D // 2), BF16),
        vmem((2, ROWS, D // 2), BF16),
        vmem((2, ROWS, D // 2), BF16),
        vmem((2, ROWS, D // 2), F32),
        vmem((2, ROWS, D // 2), F32),
        dma((2,)),
        dma((2, 2, NY, 2)), dma((2, 2, NY, 2)),
        dma((2,)),
        dma((NZ, H, 2)), dma((NZ, H, 2)), dma((H, 2)),
        dma((NX, H, 2)), dma((NX, H, 2)), dma((2, H, 2, 2)),
        dma((NZ, H, 2)), dma((NZ, H, 2)),
        dma((NZ, H, 2)), dma((NZ, H, 2)),
        dma((2,)), dma((2,)),
        dma((2, 2, NY)), dma((2, 2, NY)),
        dma((2,)), dma((2,)),
        dma((2,)), dma((2,)),
    ]
    held = pl.BlockSpec(memory_space=pltpu.VMEM)
    left = pl.BlockSpec(memory_space=pl.ANY)
    return pl.pallas_call(
        kernel,
        out_shape=jax.ShapeDtypeStruct(latent.shape, F32),
        in_specs=[held, held, left, left],
        out_specs=held,
        scratch_shapes=scratch,
        compiler_params=pltpu.CompilerParams(
            collective_id=0, has_side_effects=True, vmem_limit_bytes=60 * 1024 * 1024
        ),
    )(latent, modulation, wq, wo)


def shards(latent, modulation, w_qkv, w_out, timestep):
    wq = jnp.transpose(w_qkv, (1, 0, 2))
    wo = w_out.reshape(H * DH, D)
    change = guided(latent, jnp.transpose(modulation, (1, 0, 2)), wq, wo)
    moment = timestep[0].astype(F32)
    sigma_now = sigma_at(moment)
    step_size = sigma_at(moment + 1.0) - sigma_now
    velocity = latent + change
    return (latent + step_size * velocity, latent - sigma_now * velocity)


def solution(mesh):
    placed = (
        P(("seq", "head"), None),
        P("branch", None, None),
        P(None, "head", None),
        P("head", None, None),
        P(),
    )
    return jax.shard_map(
        shards,
        mesh=mesh,
        in_specs=placed,
        out_specs=(P(("seq", "head"), None), P(("seq", "head"), None)),
        check_vma=False,
    )
```

```python
import functools

import jax
import jax.numpy as jnp
from jax import lax
from jax.experimental import pallas as pl
from jax.experimental.pallas import tpu as pltpu
from jax.sharding import PartitionSpec as P

STEPS = 50
GUIDANCE = 6.0
SHIFT = 7.0
EPS = 1e-06
LOG2E = 1.4426950408889634
MESH = pl.DeviceIdType.MESH
F32, BF16 = jnp.float32, jnp.bfloat16

D = 3072
DH = 128
H = 3
NX, NY, NZ = 4, 4, 4
ROWS = 32
PART = ROWS // 2
CHUNK = 2 * NY * PART
WIDE = D // 2
YD = (1, 3, 2)
ZD = (2, 3, 1)


def sigma_at(step_value):
    fraction = 1.0 - step_value / STEPS
    return SHIFT * fraction / (1.0 + (SHIFT - 1.0) * fraction)


def toggled(z, k):
    if k == 1:
        return z + 1 - 2 * (z % 2)
    if k == 2:
        return z + 2 - 4 * (z // 2)
    return 3 - z


def kernel(
    lat_ref, mod_ref, wq_hbm, wo_hbm, out_ref,
    wq, wo, xh, nm, qb, kv, osend, orecv, lsend, lrecv, att, attx, gate, gatex,
    psend, precv, zsend, zrecv, fin, finx,
    w_sem, xs_sem, xr_sem, x2_sem, g_sem, qs_sem, qr_sem, q3_sem, ks_sem, kr_sem, k2_sem,
    os_sem, or_sem, ls_sem, lr_sem, as_sem, ar_sem, ps_sem, pr_sem, zs_sem, zr_sem, fs_sem, fr_sem,
):
    b, s, h = lax.axis_index("branch"), lax.axis_index("seq"), lax.axis_index("head")
    x, z, y, zh = s // NZ, s % NZ, h // 2, h % 2

    def to_y(d):
        return (b, s, ((y + d) % NY) * 2 + zh)

    def to_x(d):
        return (b, ((x + d) % NX) * NZ + z, h)

    def to_z(k):
        return (b, x * NZ + toggled(z, k), h)

    far = (b, s, h + 1 - 2 * zh)
    twin = (1 - b, s, h)
    inner = (z == 1) | (z == 2)

    def remote(src, dst, ssem, rsem, dev):
        return pltpu.make_async_remote_copy(
            src_ref=src, dst_ref=dst, send_sem=ssem, recv_sem=rsem,
            device_id=dev, device_id_type=MESH,
        )

    load_q = pltpu.make_async_copy(wq_hbm, wq, w_sem.at[0])
    load_o = pltpu.make_async_copy(wo_hbm, wo, w_sem.at[1])
    load_q.start()
    load_o.start()

    barrier = pltpu.get_barrier_semaphore()
    peers = [to_y(d) for d in YD] + [to_x(d) for d in (1, 3)] + [to_z(k) for k in ZD] + [far, twin]
    for dev in peers:
        pl.semaphore_signal(barrier, inc=1, device_id=dev, device_id_type=MESH)

    def normalise(at):
        rows = lat_ref[pl.ds(pl.multiple_of(at * ROWS, ROWS), ROWS), :]
        centred = rows - jnp.mean(rows, axis=1, keepdims=True)
        var = jnp.mean(centred * centred, axis=1, keepdims=True)
        return (centred * lax.rsqrt(var + EPS)).astype(BF16).reshape(2, PART, D)

    xh[0, :, 0, 0] = normalise(b)
    weight = jnp.where(b == 0, GUIDANCE, 1.0 - GUIDANCE).astype(F32)
    gate[...] = jnp.broadcast_to(weight * mod_ref[2], gate.shape)
    pl.semaphore_wait(barrier, len(peers))

    sends = []

    def go(copy):
        copy.start()
        sends.append(copy)
        return copy

    def x_copy(src, dst, dev):
        return go(remote(xh.at[src], xh.at[dst], xs_sem.at[dst], xr_sem.at[dst], dev))

    def modulate(dz, c, half, dy):
        rows = pl.ds(((c * 2 + half) * NY + dy) * PART, PART)
        nm[dz, rows, :] = (xh[dz, c, half, dy].astype(F32) * (1.0 + mod_ref[1]) + mod_ref[0]).astype(BF16)

    x_in = {}

    def spread(dz, c):
        for d in (1, 3):
            x_in[dz, c, 0, d] = x_copy((dz, c, 0, 0), (dz, c, 0, d), to_y(d))

    def pass_on(dz, d, c):
        x_in[dz, c, 0, d].wait_recv()
        side = d // 2
        cols = pl.ds(side * WIDE, WIDE)
        x_in[dz, c, 0, 2, side] = go(
            remote(
                xh.at[dz, c, 0, d, :, cols],
                xh.at[dz, c, 0, 2, :, cols],
                x2_sem.at[0, dz, c, side],
                x2_sem.at[1, dz, c, side],
                to_y(d),
            )
        )
        x_in[dz, c, 1, d] = x_copy((dz, c, 0, d), (dz, c, 1, d), twin)
        modulate(dz, c, 0, d)

    def pass_last(dz, c):
        for side in range(2):
            x_in[dz, c, 0, 2, side].wait_recv()
        x_in[dz, c, 1, 2] = x_copy((dz, c, 0, 2), (dz, c, 1, 2), twin)
        modulate(dz, c, 0, 2)

    def from_far(c):
        x_in[1, c, 0, 0].wait_recv()
        spread(1, c)
        x_in[1, c, 1, 0] = x_copy((1, c, 0, 0), (1, c, 1, 0), twin)
        modulate(1, c, 0, 0)

    def from_twin(dz, c):
        for dy in (0, 1, 3, 2):
            if (dz, dy) != (0, 0):
                x_in[dz, c, 1, dy].wait_recv()
                modulate(dz, c, 1, dy)

    for c in range(2):
        x_in[1, c, 0, 0] = x_copy((0, c, 0, 0), (1, c, 0, 0), far)
        spread(0, c)
    gate_copy = go(remote(gate, gatex, g_sem.at[0], g_sem.at[1], twin))
    xh[0, :, 1, 0] = normalise(1 - b)
    for c in range(2):
        modulate(0, c, 0, 0)
        modulate(0, c, 1, 0)

    def piece(ref, m):
        return ref.at[0, m] if m < 2 else ref.at[1 if m == 2 else 0]

    def rows_of(m):
        return CHUNK if m < 2 else 2 * CHUNK

    def parts_of(m):
        return (m,) if m < 2 else (0, 1)

    q_scale = DH**-0.5 * LOG2E
    q_in, kv_in = {}, {}

    def project(m):
        dz = m // 2
        parts = (m,) if m < 2 else (0, 1)
        rows = slice(m * CHUNK, (m + 1) * CHUNK) if m < 2 else slice(0, 2 * CHUNK)
        for i in range(H):
            got = jnp.dot(nm[dz, rows], wq[i, :, DH:], preferred_element_type=F32)
            for at, c in enumerate(parts):
                mine = got[at * CHUNK : (at + 1) * CHUNK]
                kv[0, i, dz, c, 0] = mine[:, :DH].T.astype(BF16)
                kv[0, i, dz, c, 1] = mine[:, DH:].astype(BF16)
            for d in (1, 3):
                at = (d, i, m)
                kv_in[at] = go(
                    remote(piece(kv.at[0, i], m), piece(kv.at[d, i], m), ks_sem.at[at], kr_sem.at[at], to_x(d))
                )
            got = jnp.dot(nm[dz, rows], wq[i, :, :DH], preferred_element_type=F32) * q_scale
            for at, c in enumerate(parts):
                qb[0, i, dz, c] = got[at * CHUNK : (at + 1) * CHUNK].astype(BF16)
            for k in (2, 1, 3):
                at = (k, i, m)
                q_in[at] = remote(piece(qb.at[0, i], m), piece(qb.at[k, i], m), qs_sem.at[at], qr_sem.at[at], to_z(k))
                if k < 3:
                    go(q_in[at])
                else:
                    pl.when(inner)(q_in[at].start)

    def relay_x(m, i):
        for d in (1, 3):
            kv_in[d, i, m].wait_recv()
            side = d // 2
            src, dst = (piece(kv.at[at, i], m).at[side] for at in (d, 2))
            kv_in[2, i, m, side] = go(
                remote(src, dst, k2_sem.at[0, i, m, side], k2_sem.at[1, i, m, side], to_x(d))
            )

    relays = []

    def relay_z(m, i):
        q_in[2, i, m].wait_recv()
        relay = remote(piece(qb.at[2, i], m), piece(qb.at[3, i], m), q3_sem.at[i, m], qr_sem.at[3, i, m], to_z(1))
        pl.when(inner)(relay.start)
        relays.append(relay)

    for c in range(2):
        pass_on(0, 1, c)
        pass_on(0, 3, c)
    from_far(0)
    pass_last(0, 0)
    from_twin(0, 0)
    load_q.wait()
    project(0)
    from_far(1)
    pass_last(0, 1)
    from_twin(0, 1)
    project(1)
    pass_on(1, 1, 0)
    pass_on(1, 3, 0)
    relay_x(0, 0)
    pass_on(1, 1, 1)
    pass_on(1, 3, 1)
    relay_x(0, 1)
    relay_x(0, 2)
    for i in range(H):
        relay_z(0, i)
    pass_last(1, 0)
    pass_last(1, 1)
    relay_x(1, 0)
    from_twin(1, 0)
    from_twin(1, 1)
    project(2)
    relay_x(1, 1)
    relay_x(1, 2)
    for i in range(H):
        relay_z(1, i)
    for i in range(H):
        relay_x(2, i)
        relay_z(2, i)

    def attend(ks, i, m):
        rows = rows_of(m)
        query = jnp.concatenate([piece(qb.at[k, i], m)[...].reshape(rows, DH) for k in ks], axis=0)
        blocks = [(d, dz) for d in range(NX) for dz in range(2)]
        scores = jnp.concatenate(
            [
                jnp.dot(
                    query,
                    jnp.concatenate([kv[d, i, dz, 0, 0], kv[d, i, dz, 1, 0]], axis=1),
                    preferred_element_type=F32,
                )
                for d, dz in blocks
            ],
            axis=1,
        )
        peak = jnp.max(scores, axis=1, keepdims=True)
        expo = jnp.exp2(scores - peak)
        total = jnp.sum(expo, axis=1, keepdims=True)
        probs = expo.astype(BF16)
        mixed = jnp.zeros((len(ks) * rows, DH), F32)
        for at, (d, dz) in enumerate(blocks):
            mixed += jnp.dot(
                probs[:, at * 2 * CHUNK : (at + 1) * 2 * CHUNK],
                jnp.concatenate([kv[d, i, dz, 0, 1], kv[d, i, dz, 1, 1]], axis=0),
                preferred_element_type=F32,
            )
        mixed = (mixed / total).astype(BF16)
        log = jnp.broadcast_to(peak + jnp.log2(total), mixed.shape).T[:8, :]
        for at, k in enumerate(ks):
            mine = slice(at * rows, (at + 1) * rows)
            out = piece(osend.at[k, i], m)
            out[...] = mixed[mine].reshape(out.shape)
            lsend[k, i, m, :, :rows] = log[:, mine]

    o_in = {}

    def send_back(k, i, m, slot, dev):
        at = (slot, i, m)
        lanes = pl.ds(0, rows_of(m))
        o_in[at] = [
            go(remote(piece(osend.at[k, i], m), piece(orecv.at[slot, i], m), os_sem.at[at], or_sem.at[at], dev)),
            go(remote(lsend.at[k, i, m, :, lanes], lrecv.at[slot, i, m, :, lanes], ls_sem.at[at], lr_sem.at[at], dev)),
        ]

    def merged(i, m, parts):
        rows = rows_of(m)
        logs = [log[i, m, :, :rows] for _, log in parts]
        peak = functools.reduce(jnp.maximum, logs)
        shares = [jnp.exp2(log - peak) for log in logs]
        total = functools.reduce(jnp.add, shares)
        mixed = jnp.zeros((rows, DH), F32)
        for share, (out, _) in zip(shares, parts):
            column = jnp.concatenate([share / total] * (DH // 8), axis=0).T
            mixed += column * piece(out.at[i], m)[...].reshape(rows, DH).astype(F32)
        return mixed.astype(BF16), peak + jnp.log2(total)

    def cross(i, m):
        for copy in o_in[3, i, m]:
            copy.wait_recv()
        mixed, log = merged(i, m, [(osend.at[2], lsend.at[2]), (orecv.at[3], lrecv.at[3])])
        out = piece(osend.at[4, i], m)
        out[...] = mixed.reshape(out.shape)
        lsend[4, i, m, :, : rows_of(m)] = log
        send_back(4, i, m, 2, to_z(2))

    a_in = {}

    def merge(i, m):
        for k in (1, 2):
            for copy in o_in[k, i, m]:
                copy.wait_recv()
        mixed, _ = merged(
            i, m, [(osend.at[0], lsend.at[0])] + [(orecv.at[k], lrecv.at[k]) for k in (1, 2)]
        )
        for at, c in enumerate(parts_of(m)):
            for half in range(2):
                first = at * CHUNK + half * CHUNK // 2
                att[half, i, int(m == 2), c] = mixed[first : first + CHUNK // 2]
        a_in[i, m] = go(
            remote(piece(att.at[1, i], m), piece(attx.at[i], m), as_sem.at[i, m], ar_sem.at[i, m], twin)
        )

    def outgoing(i, m):
        for k in (3, 1):
            for n in (0, 1) if m == 3 else (m,):
                q_in[k, i, n].wait_recv()
        for ks in ((3,), (1,)):
            attend(ks, i, m)
            for k in ks:
                send_back(k, i, m, k, to_z(1))

    def staying(i, m):
        for ks in ((2, 0),) if m >= 2 else ((2,), (0,)):
            attend(ks, i, m)

    p_in = {}
    tile = 512

    def project_out(m):
        for i in range(H):
            n = 3 if m < 2 and i < H - 1 else m
            if (n, m) != (3, 1):
                a_in[i, n].wait_recv()
        rows = rows_of(m) // 2
        both = jnp.concatenate(
            [
                jnp.concatenate([piece(ref.at[i], m)[...].reshape(rows, DH) for i in range(H)], axis=1)
                for ref in (att.at[0], attx)
            ],
            axis=0,
        )
        for side in range(2):
            for t in range(WIDE // tile):
                cols = slice(side * WIDE + t * tile, side * WIDE + (t + 1) * tile)
                got = jnp.dot(both, wo[:, cols], preferred_element_type=F32)
                got = (gate[0:1, cols] * got[:rows] + gatex[0:1, cols] * got[rows:]).astype(BF16)
                for at, c in enumerate((m,) if m < 2 else (0, 1)):
                    mine = got[at * CHUNK // 2 : (at + 1) * CHUNK // 2].reshape(NY, PART, tile)
                    psend[side, :, m // 2, c, :, t * tile : (t + 1) * tile] = mine
            for d in (2, 1, 3):
                at = (m, side, d)
                p_in[at] = go(
                    remote(
                        piece(psend.at[side, d], m), piece(precv.at[side, d], m), ps_sem.at[at], pr_sem.at[at], to_y(NY - d)
                    )
                )

    def summed(m, side):
        total = piece(psend.at[side, 0], m)[...].astype(F32)
        for d in (1, 3, 2):
            p_in[m, side, d].wait_recv()
            total += piece(precv.at[side, d], m)[...].astype(F32)
        return total

    def arrived(i):
        for m in range(3):
            for side in range(2):
                kv_in[2, i, m, side].wait_recv()

    def ready():
        load_o.wait()
        gate_copy.wait_recv()

    steps = [(0, 2), (1, 2), (2, 2), (0, 3), (1, 3), (2, 0), (2, 1)]
    during = {(2, 0): [lambda: project_out(2)]}
    after = {
        (0, 3): [lambda: merge(0, 2), lambda: merge(1, 2)],
        (1, 3): [ready, lambda: merge(2, 2)],
        (2, 0): [lambda: merge(0, 3)],
        (2, 1): [lambda: merge(1, 3)],
    }
    for at, (i, m) in enumerate(steps):
        if m == 2:
            arrived(i)
        outgoing(i, m)
        if at:
            cross(*steps[at - 1])
        for task in during.get((i, m), []):
            task()
        staying(i, m)
        for task in after.get((i, m), []):
            task()
    merge(2, 0)
    cross(*steps[-1])
    project_out(0)

    z_in, f_in = [], {}
    for side in range(2):
        zsend[side] = summed(2, side).astype(BF16)
        z_in.append(go(remote(zsend.at[side], zrecv.at[side], zs_sem.at[side], zr_sem.at[side], far)))
    merge(2, 1)
    project_out(1)
    for m in range(2):
        for side in range(2):
            whole = summed(m, side)
            if m == 0:
                z_in[side].wait_recv()
            whole += zrecv[side, m].astype(F32)
            fin[m, side] = whole
            f_in[m, side] = go(
                remote(fin.at[m, side], finx.at[m, side], fs_sem.at[m, side], fr_sem.at[m, side], twin)
            )
            rows = pl.ds(pl.multiple_of(b * ROWS + m * PART, PART), PART)
            out_ref[rows, side * WIDE : (side + 1) * WIDE] = whole
    for m in range(2):
        for side in range(2):
            f_in[m, side].wait_recv()
            rows = pl.ds(pl.multiple_of((1 - b) * ROWS + m * PART, PART), PART)
            out_ref[rows, side * WIDE : (side + 1) * WIDE] = finx[m, side]

    for copy in sends:
        copy.wait_send()

    @pl.when(inner)
    def _():
        for copy in relays:
            copy.wait_send()
        for m in range(3):
            for i in range(H):
                q_in[3, i, m].wait_send()


def guided(latent, modulation, wq, wo):
    dma = pltpu.SemaphoreType.DMA
    vmem = pltpu.VMEM
    scratch = [
        vmem((H, D, 3 * DH), BF16),
        vmem((H * DH, D), BF16),
        vmem((2, 2, 2, NY, PART, D), BF16),
        vmem((2, 2 * CHUNK, D), BF16),
        vmem((NZ, H, 2, 2, CHUNK, DH), BF16),
        vmem((NX, H, 2, 2, 2, DH, CHUNK), BF16),
        vmem((NZ + 1, H, 2, 2, CHUNK, DH), BF16),
        vmem((NZ, H, 2, 2, CHUNK, DH), BF16),
        vmem((NZ + 1, H, 4, 8, 2 * CHUNK), F32),
        vmem((NZ, H, 4, 8, 2 * CHUNK), F32),
        vmem((2, H, 2, 2, CHUNK // 2, DH), BF16),
        vmem((H, 2, 2, CHUNK // 2, DH), BF16),
        vmem((8, D), F32),
        vmem((8, D), F32),
        vmem((2, NY, 2, 2, PART, WIDE), BF16),
        vmem((2, NY, 2, 2, PART, WIDE), BF16),
        vmem((2, 2, PART, WIDE), BF16),
        vmem((2, 2, PART, WIDE), BF16),
        vmem((2, 2, PART, WIDE), F32),
        vmem((2, 2, PART, WIDE), F32),
        dma((2,)),
        dma((2, 2, 2, NY)), dma((2, 2, 2, NY)), dma((2, 2, 2, 2)),
        dma((2,)),
        dma((NZ, H, 3)), dma((NZ, H, 3)), dma((H, 3)),
        dma((NX, H, 3)), dma((NX, H, 3)), dma((2, H, 3, 2)),
        dma((NZ, H, 4)), dma((NZ, H, 4)),
        dma((NZ, H, 4)), dma((NZ, H, 4)),
        dma((H, 4)), dma((H, 4)),
        dma((3, 2, NY)), dma((3, 2, NY)),
        dma((2,)), dma((2,)),
        dma((2, 2)), dma((2, 2)),
    ]
    held = pl.BlockSpec(memory_space=pltpu.VMEM)
    left = pl.BlockSpec(memory_space=pl.ANY)
    return pl.pallas_call(
        kernel,
        out_shape=jax.ShapeDtypeStruct(latent.shape, F32),
        in_specs=[held, held, left, left],
        out_specs=held,
        scratch_shapes=scratch,
        compiler_params=pltpu.CompilerParams(
            collective_id=0, has_side_effects=True, vmem_limit_bytes=60 * 1024 * 1024
        ),
    )(latent, modulation, wq, wo)


def shards(latent, modulation, w_qkv, w_out, timestep):
    wq = jnp.transpose(w_qkv, (1, 0, 2))
    wo = w_out.reshape(H * DH, D)
    change = guided(latent, jnp.transpose(modulation, (1, 0, 2)), wq, wo)
    moment = timestep[0].astype(F32)
    sigma_now = sigma_at(moment)
    step_size = sigma_at(moment + 1.0) - sigma_now
    velocity = latent + change
    return (latent + step_size * velocity, latent - sigma_now * velocity)


def solution(mesh):
    placed = (
        P(("seq", "head"), None),
        P("branch", None, None),
        P(None, "head", None),
        P("head", None, None),
        P(),
    )
    return jax.shard_map(
        shards,
        mesh=mesh,
        in_specs=placed,
        out_specs=(P(("seq", "head"), None), P(("seq", "head"), None)),
        check_vma=False,
    )
```

```python
import functools

import jax
import jax.numpy as jnp
from jax import lax
from jax.experimental import pallas as pl
from jax.experimental.pallas import tpu as pltpu
from jax.sharding import PartitionSpec as P

STEPS = 50
GUIDANCE = 6.0
SHIFT = 7.0
EPS = 1e-06
LOG2E = 1.4426950408889634
MESH = pl.DeviceIdType.MESH
F32, BF16 = jnp.float32, jnp.bfloat16

D = 3072
DH = 128
H = 3
NX, NY, NZ = 4, 4, 4
ROWS = 32
PART = ROWS // 2
CHUNK = 2 * NY * PART
WIDE = D // 2
YD = (1, 3, 2)
ZD = (2, 3, 1)


def sigma_at(step_value):
    fraction = 1.0 - step_value / STEPS
    return SHIFT * fraction / (1.0 + (SHIFT - 1.0) * fraction)


def toggled(z, k):
    if k == 1:
        return z + 1 - 2 * (z % 2)
    if k == 2:
        return z + 2 - 4 * (z // 2)
    return 3 - z


def kernel(
    lat_ref, mod_ref, wq_hbm, wo_hbm, out_ref,
    wq, wo, xh, nm, qb, kv, osend, orecv, lsend, lrecv, att, attx, gate, gatex,
    psend, precv, zsend, zrecv, fin, finx,
    w_sem, xs_sem, xr_sem, x2_sem, g_sem, qs_sem, qr_sem, q3_sem, ks_sem, kr_sem, k2_sem,
    os_sem, or_sem, ls_sem, lr_sem, as_sem, ar_sem, ps_sem, pr_sem, zs_sem, zr_sem, fs_sem, fr_sem,
):
    b, s, h = lax.axis_index("branch"), lax.axis_index("seq"), lax.axis_index("head")
    x, z, y, zh = s // NZ, s % NZ, h // 2, h % 2

    def to_y(d):
        return (b, s, ((y + d) % NY) * 2 + zh)

    def to_x(d):
        return (b, ((x + d) % NX) * NZ + z, h)

    def to_z(k):
        return (b, x * NZ + toggled(z, k), h)

    far = (b, s, h + 1 - 2 * zh)
    twin = (1 - b, s, h)
    inner = (z == 1) | (z == 2)

    def remote(src, dst, ssem, rsem, dev):
        return pltpu.make_async_remote_copy(
            src_ref=src, dst_ref=dst, send_sem=ssem, recv_sem=rsem,
            device_id=dev, device_id_type=MESH,
        )

    load_q = pltpu.make_async_copy(wq_hbm, wq, w_sem.at[0])
    load_o = pltpu.make_async_copy(wo_hbm, wo, w_sem.at[1])
    load_q.start()
    load_o.start()

    barrier = pltpu.get_barrier_semaphore()
    peers = [to_y(d) for d in YD] + [to_x(d) for d in (1, 3)] + [to_z(k) for k in ZD] + [far, twin]
    for dev in peers:
        pl.semaphore_signal(barrier, inc=1, device_id=dev, device_id_type=MESH)

    def normalise(at):
        rows = lat_ref[pl.ds(pl.multiple_of(at * ROWS, ROWS), ROWS), :]
        centred = rows - jnp.mean(rows, axis=1, keepdims=True)
        var = jnp.mean(centred * centred, axis=1, keepdims=True)
        return (centred * lax.rsqrt(var + EPS)).astype(BF16).reshape(2, PART, D)

    xh[0, :, 0, 0] = normalise(b)
    weight = jnp.where(b == 0, GUIDANCE, 1.0 - GUIDANCE).astype(F32)
    gate[...] = jnp.broadcast_to(weight * mod_ref[2], gate.shape)
    pl.semaphore_wait(barrier, len(peers))

    sends = []

    def go(copy):
        copy.start()
        sends.append(copy)
        return copy

    def x_copy(src, dst, dev):
        return go(remote(xh.at[src], xh.at[dst], xs_sem.at[dst], xr_sem.at[dst], dev))

    def modulate(dz, c, half, dy):
        rows = pl.ds(((c * 2 + half) * NY + dy) * PART, PART)

        def some(t, carry):
            cols = pl.ds(pl.multiple_of(t * tile, tile), tile)
            nm[dz, rows, cols] = (
                xh[dz, c, half, dy, :, cols].astype(F32) * (1.0 + mod_ref[1, :, cols]) + mod_ref[0, :, cols]
            ).astype(BF16)
            return carry

        lax.fori_loop(0, D // tile, some, 0)

    tile = 512
    x_in = {}

    def spread(dz, c):
        for d in (1, 3):
            x_in[dz, c, 0, d] = x_copy((dz, c, 0, 0), (dz, c, 0, d), to_y(d))

    def pass_on(dz, d, c):
        x_in[dz, c, 0, d].wait_recv()
        side = d // 2
        cols = pl.ds(side * WIDE, WIDE)
        x_in[dz, c, 0, 2, side] = go(
            remote(
                xh.at[dz, c, 0, d, :, cols],
                xh.at[dz, c, 0, 2, :, cols],
                x2_sem.at[0, dz, c, side],
                x2_sem.at[1, dz, c, side],
                to_y(d),
            )
        )
        x_in[dz, c, 1, d] = x_copy((dz, c, 0, d), (dz, c, 1, d), twin)
        modulate(dz, c, 0, d)

    def pass_last(dz, c):
        for side in range(2):
            x_in[dz, c, 0, 2, side].wait_recv()
        x_in[dz, c, 1, 2] = x_copy((dz, c, 0, 2), (dz, c, 1, 2), twin)
        modulate(dz, c, 0, 2)

    def from_far(c):
        x_in[1, c, 0, 0].wait_recv()
        spread(1, c)
        x_in[1, c, 1, 0] = x_copy((1, c, 0, 0), (1, c, 1, 0), twin)
        modulate(1, c, 0, 0)

    def from_twin(dz, c):
        for dy in (0, 1, 3, 2):
            if (dz, dy) != (0, 0):
                x_in[dz, c, 1, dy].wait_recv()
                modulate(dz, c, 1, dy)

    for c in range(2):
        x_in[1, c, 0, 0] = x_copy((0, c, 0, 0), (1, c, 0, 0), far)
        spread(0, c)
    gate_copy = go(remote(gate, gatex, g_sem.at[0], g_sem.at[1], twin))
    xh[0, :, 1, 0] = normalise(1 - b)
    for c in range(2):
        modulate(0, c, 0, 0)
        modulate(0, c, 1, 0)

    def piece(ref, m):
        return ref.at[0, m] if m < 2 else ref.at[1 if m == 2 else 0]

    def rows_of(m):
        return CHUNK if m < 2 else 2 * CHUNK

    def parts_of(m):
        return (m,) if m < 2 else (0, 1)

    q_scale = DH**-0.5 * LOG2E
    q_in, kv_in = {}, {}

    def project(m):
        dz = m // 2
        parts = (m,) if m < 2 else (0, 1)
        rows = slice(m * CHUNK, (m + 1) * CHUNK) if m < 2 else slice(0, 2 * CHUNK)

        def to_neighbours(i):
            return [
                remote(piece(kv.at[0, i], m), piece(kv.at[d, i], m), ks_sem.at[d, i, m], kr_sem.at[d, i, m], to_x(d))
                for d in (1, 3)
            ]

        def along_line(i):
            return [
                remote(piece(qb.at[0, i], m), piece(qb.at[k, i], m), qs_sem.at[k, i, m], qr_sem.at[k, i, m], to_z(k))
                for k in (2, 1, 3)
            ]

        def per_head(i, carry):
            got = jnp.dot(nm[dz, rows], wq[i, :, DH:], preferred_element_type=F32)
            for at, c in enumerate(parts):
                mine = got[at * CHUNK : (at + 1) * CHUNK]
                kv[0, i, dz, c, 0] = mine[:, :DH].T.astype(BF16)
                kv[0, i, dz, c, 1] = mine[:, DH:].astype(BF16)
            for copy in to_neighbours(i):
                copy.start()
            got = jnp.dot(nm[dz, rows], wq[i, :, :DH], preferred_element_type=F32) * q_scale
            for at, c in enumerate(parts):
                qb[0, i, dz, c] = got[at * CHUNK : (at + 1) * CHUNK].astype(BF16)
            across, near, between = along_line(i)
            across.start()
            near.start()
            pl.when(inner)(between.start)
            return carry

        lax.fori_loop(0, H, per_head, 0)
        for i in range(H):
            kv_in[1, i, m], kv_in[3, i, m] = to_neighbours(i)
            q_in[2, i, m], q_in[1, i, m], q_in[3, i, m] = along_line(i)
            sends.extend([kv_in[1, i, m], kv_in[3, i, m], q_in[2, i, m], q_in[1, i, m]])

    def relay_x(m, i):
        for d in (1, 3):
            kv_in[d, i, m].wait_recv()
            side = d // 2
            src, dst = (piece(kv.at[at, i], m).at[side] for at in (d, 2))
            kv_in[2, i, m, side] = go(
                remote(src, dst, k2_sem.at[0, i, m, side], k2_sem.at[1, i, m, side], to_x(d))
            )

    relays = []

    def relay_z(m, i):
        q_in[2, i, m].wait_recv()
        relay = remote(piece(qb.at[2, i], m), piece(qb.at[3, i], m), q3_sem.at[i, m], qr_sem.at[3, i, m], to_z(1))
        pl.when(inner)(relay.start)
        relays.append(relay)

    for c in range(2):
        pass_on(0, 1, c)
        pass_on(0, 3, c)
    from_far(0)
    pass_last(0, 0)
    from_twin(0, 0)
    load_q.wait()
    project(0)
    from_far(1)
    pass_last(0, 1)
    from_twin(0, 1)
    project(1)
    pass_on(1, 1, 0)
    pass_on(1, 3, 0)
    relay_x(0, 0)
    pass_on(1, 1, 1)
    pass_on(1, 3, 1)
    relay_x(0, 1)
    relay_x(0, 2)
    for i in range(H):
        relay_z(0, i)
    pass_last(1, 0)
    pass_last(1, 1)
    relay_x(1, 0)
    from_twin(1, 0)
    from_twin(1, 1)
    project(2)
    relay_x(1, 1)
    relay_x(1, 2)
    for i in range(H):
        relay_z(1, i)
    for i in range(H):
        relay_x(2, i)
        relay_z(2, i)

    def attend(ks, i, m):
        rows = rows_of(m)
        query = jnp.concatenate([piece(qb.at[k, i], m)[...].reshape(rows, DH) for k in ks], axis=0)
        blocks = [(d, dz) for d in range(NX) for dz in range(2)]
        scores = jnp.concatenate(
            [
                jnp.dot(
                    query,
                    jnp.concatenate([kv[d, i, dz, 0, 0], kv[d, i, dz, 1, 0]], axis=1),
                    preferred_element_type=F32,
                )
                for d, dz in blocks
            ],
            axis=1,
        )
        peak = jnp.max(scores, axis=1, keepdims=True)
        expo = jnp.exp2(scores - peak)
        total = jnp.sum(expo, axis=1, keepdims=True)
        probs = expo.astype(BF16)
        mixed = jnp.zeros((len(ks) * rows, DH), F32)
        for at, (d, dz) in enumerate(blocks):
            mixed += jnp.dot(
                probs[:, at * 2 * CHUNK : (at + 1) * 2 * CHUNK],
                jnp.concatenate([kv[d, i, dz, 0, 1], kv[d, i, dz, 1, 1]], axis=0),
                preferred_element_type=F32,
            )
        mixed = (mixed / total).astype(BF16)
        log = jnp.broadcast_to(peak + jnp.log2(total), mixed.shape).T[:8, :]
        for at, k in enumerate(ks):
            mine = slice(at * rows, (at + 1) * rows)
            out = piece(osend.at[k, i], m)
            out[...] = mixed[mine].reshape(out.shape)
            lsend[k, i, m, :, :rows] = log[:, mine]

    o_in = {}

    def send_back(k, i, m, slot, dev):
        at = (slot, i, m)
        lanes = pl.ds(0, rows_of(m))
        o_in[at] = [
            go(remote(piece(osend.at[k, i], m), piece(orecv.at[slot, i], m), os_sem.at[at], or_sem.at[at], dev)),
            go(remote(lsend.at[k, i, m, :, lanes], lrecv.at[slot, i, m, :, lanes], ls_sem.at[at], lr_sem.at[at], dev)),
        ]

    def merged(i, m, parts):
        rows = rows_of(m)
        logs = [log[i, m, :, :rows] for _, log in parts]
        peak = functools.reduce(jnp.maximum, logs)
        shares = [jnp.exp2(log - peak) for log in logs]
        total = functools.reduce(jnp.add, shares)
        mixed = jnp.zeros((rows, DH), F32)
        for share, (out, _) in zip(shares, parts):
            column = jnp.concatenate([share / total] * (DH // 8), axis=0).T
            mixed += column * piece(out.at[i], m)[...].reshape(rows, DH).astype(F32)
        return mixed.astype(BF16), peak + jnp.log2(total)

    def cross(i, m):
        for copy in o_in[3, i, m]:
            copy.wait_recv()
        mixed, log = merged(i, m, [(osend.at[2], lsend.at[2]), (orecv.at[3], lrecv.at[3])])
        out = piece(osend.at[4, i], m)
        out[...] = mixed.reshape(out.shape)
        lsend[4, i, m, :, : rows_of(m)] = log
        send_back(4, i, m, 2, to_z(2))

    a_in = {}

    def merge(i, m):
        for k in (1, 2):
            for copy in o_in[k, i, m]:
                copy.wait_recv()
        mixed, _ = merged(
            i, m, [(osend.at[0], lsend.at[0])] + [(orecv.at[k], lrecv.at[k]) for k in (1, 2)]
        )
        for at, c in enumerate(parts_of(m)):
            for half in range(2):
                first = at * CHUNK + half * CHUNK // 2
                att[half, i, int(m == 2), c] = mixed[first : first + CHUNK // 2]
        a_in[i, m] = go(
            remote(piece(att.at[1, i], m), piece(attx.at[i], m), as_sem.at[i, m], ar_sem.at[i, m], twin)
        )

    def outgoing(i, m):
        for k in (3, 1):
            for n in (0, 1) if m == 3 else (m,):
                q_in[k, i, n].wait_recv()
        for ks in ((3,), (1,)):
            attend(ks, i, m)
            for k in ks:
                send_back(k, i, m, k, to_z(1))

    def staying(i, m):
        for ks in ((2, 0),) if m >= 2 else ((2,), (0,)):
            attend(ks, i, m)

    p_in = {}

    def project_out(m):
        for i in range(H):
            n = 3 if m < 2 and i < H - 1 else m
            if (n, m) != (3, 1):
                a_in[i, n].wait_recv()
        rows = rows_of(m) // 2
        both = jnp.concatenate(
            [
                jnp.concatenate([piece(ref.at[i], m)[...].reshape(rows, DH) for i in range(H)], axis=1)
                for ref in (att.at[0], attx)
            ],
            axis=0,
        )
        for side in range(2):

            def some(t, carry, side=side):
                cols = pl.ds(pl.multiple_of(side * WIDE + t * tile, tile), tile)
                got = jnp.dot(both, wo[:, cols], preferred_element_type=F32)
                got = (gate[0:1, cols] * got[:rows] + gatex[0:1, cols] * got[rows:]).astype(BF16)
                for at, c in enumerate(parts_of(m)):
                    mine = got[at * CHUNK // 2 : (at + 1) * CHUNK // 2].reshape(NY, PART, tile)
                    psend[side, :, m // 2, c, :, pl.ds(pl.multiple_of(t * tile, tile), tile)] = mine
                return carry

            lax.fori_loop(0, WIDE // tile, some, 0)
            for d in (2, 1, 3):
                at = (m, side, d)
                p_in[at] = go(
                    remote(
                        piece(psend.at[side, d], m), piece(precv.at[side, d], m), ps_sem.at[at], pr_sem.at[at], to_y(NY - d)
                    )
                )

    def summed(m, side):
        total = piece(psend.at[side, 0], m)[...].astype(F32)
        for d in (1, 3, 2):
            p_in[m, side, d].wait_recv()
            total += piece(precv.at[side, d], m)[...].astype(F32)
        return total

    def arrived(i):
        for m in range(3):
            for side in range(2):
                kv_in[2, i, m, side].wait_recv()

    def ready():
        load_o.wait()
        gate_copy.wait_recv()

    steps = [(0, 2), (1, 2), (2, 2), (0, 3), (1, 3), (2, 0), (2, 1)]
    during = {(2, 0): [lambda: project_out(2)]}
    after = {
        (0, 3): [lambda: merge(0, 2), lambda: merge(1, 2)],
        (1, 3): [ready, lambda: merge(2, 2)],
        (2, 0): [lambda: merge(0, 3)],
        (2, 1): [lambda: merge(1, 3)],
    }
    for at, (i, m) in enumerate(steps):
        if m == 2:
            arrived(i)
        outgoing(i, m)
        if at:
            cross(*steps[at - 1])
        for task in during.get((i, m), []):
            task()
        staying(i, m)
        for task in after.get((i, m), []):
            task()
    merge(2, 0)
    cross(*steps[-1])
    project_out(0)

    z_in, f_in = [], {}
    for side in range(2):
        zsend[side] = summed(2, side).astype(BF16)
        z_in.append(go(remote(zsend.at[side], zrecv.at[side], zs_sem.at[side], zr_sem.at[side], far)))
    merge(2, 1)
    project_out(1)
    for m in range(2):
        for side in range(2):
            whole = summed(m, side)
            if m == 0:
                z_in[side].wait_recv()
            whole += zrecv[side, m].astype(F32)
            fin[m, side] = whole
            f_in[m, side] = go(
                remote(fin.at[m, side], finx.at[m, side], fs_sem.at[m, side], fr_sem.at[m, side], twin)
            )
            rows = pl.ds(pl.multiple_of(b * ROWS + m * PART, PART), PART)
            out_ref[rows, side * WIDE : (side + 1) * WIDE] = whole
    for m in range(2):
        for side in range(2):
            f_in[m, side].wait_recv()
            rows = pl.ds(pl.multiple_of((1 - b) * ROWS + m * PART, PART), PART)
            out_ref[rows, side * WIDE : (side + 1) * WIDE] = finx[m, side]

    for copy in sends:
        copy.wait_send()

    @pl.when(inner)
    def _():
        for copy in relays:
            copy.wait_send()
        for m in range(3):
            for i in range(H):
                q_in[3, i, m].wait_send()


def guided(latent, modulation, wq, wo):
    dma = pltpu.SemaphoreType.DMA
    vmem = pltpu.VMEM
    scratch = [
        vmem((H, D, 3 * DH), BF16),
        vmem((H * DH, D), BF16),
        vmem((2, 2, 2, NY, PART, D), BF16),
        vmem((2, 2 * CHUNK, D), BF16),
        vmem((NZ, H, 2, 2, CHUNK, DH), BF16),
        vmem((NX, H, 2, 2, 2, DH, CHUNK), BF16),
        vmem((NZ + 1, H, 2, 2, CHUNK, DH), BF16),
        vmem((NZ, H, 2, 2, CHUNK, DH), BF16),
        vmem((NZ + 1, H, 4, 8, 2 * CHUNK), F32),
        vmem((NZ, H, 4, 8, 2 * CHUNK), F32),
        vmem((2, H, 2, 2, CHUNK // 2, DH), BF16),
        vmem((H, 2, 2, CHUNK // 2, DH), BF16),
        vmem((8, D), F32),
        vmem((8, D), F32),
        vmem((2, NY, 2, 2, PART, WIDE), BF16),
        vmem((2, NY, 2, 2, PART, WIDE), BF16),
        vmem((2, 2, PART, WIDE), BF16),
        vmem((2, 2, PART, WIDE), BF16),
        vmem((2, 2, PART, WIDE), F32),
        vmem((2, 2, PART, WIDE), F32),
        dma((2,)),
        dma((2, 2, 2, NY)), dma((2, 2, 2, NY)), dma((2, 2, 2, 2)),
        dma((2,)),
        dma((NZ, H, 3)), dma((NZ, H, 3)), dma((H, 3)),
        dma((NX, H, 3)), dma((NX, H, 3)), dma((2, H, 3, 2)),
        dma((NZ, H, 4)), dma((NZ, H, 4)),
        dma((NZ, H, 4)), dma((NZ, H, 4)),
        dma((H, 4)), dma((H, 4)),
        dma((3, 2, NY)), dma((3, 2, NY)),
        dma((2,)), dma((2,)),
        dma((2, 2)), dma((2, 2)),
    ]
    held = pl.BlockSpec(memory_space=pltpu.VMEM)
    left = pl.BlockSpec(memory_space=pl.ANY)
    return pl.pallas_call(
        kernel,
        out_shape=jax.ShapeDtypeStruct(latent.shape, F32),
        in_specs=[held, held, left, left],
        out_specs=held,
        scratch_shapes=scratch,
        compiler_params=pltpu.CompilerParams(
            collective_id=0, has_side_effects=True, vmem_limit_bytes=60 * 1024 * 1024
        ),
    )(latent, modulation, wq, wo)


def shards(latent, modulation, w_qkv, w_out, timestep):
    wq = jnp.transpose(w_qkv, (1, 0, 2))
    wo = w_out.reshape(H * DH, D)
    change = guided(latent, jnp.transpose(modulation, (1, 0, 2)), wq, wo)
    moment = timestep[0].astype(F32)
    sigma_now = sigma_at(moment)
    step_size = sigma_at(moment + 1.0) - sigma_now
    velocity = latent + change
    return (latent + step_size * velocity, latent - sigma_now * velocity)


def solution(mesh):
    placed = (
        P(("seq", "head"), None),
        P("branch", None, None),
        P(None, "head", None),
        P("head", None, None),
        P(),
    )
    return jax.shard_map(
        shards,
        mesh=mesh,
        in_specs=placed,
        out_specs=(P(("seq", "head"), None), P(("seq", "head"), None)),
        check_vma=False,
    )
```

```python
import functools

import jax
import jax.numpy as jnp
from jax import lax
from jax.experimental import pallas as pl
from jax.experimental.pallas import tpu as pltpu
from jax.sharding import PartitionSpec as P

STEPS = 50
GUIDANCE = 6.0
SHIFT = 7.0
EPS = 1e-06
LOG2E = 1.4426950408889634
MESH = pl.DeviceIdType.MESH
F32, BF16 = jnp.float32, jnp.bfloat16

D = 3072
DH = 128
H = 3
NX, NY, NZ = 4, 4, 4
ROWS = 32
PART = ROWS // 2
CHUNK = 2 * NY * PART
WIDE = D // 2
YD = (1, 3, 2)
ZD = (2, 3, 1)


def sigma_at(step_value):
    fraction = 1.0 - step_value / STEPS
    return SHIFT * fraction / (1.0 + (SHIFT - 1.0) * fraction)


def toggled(z, k):
    if k == 1:
        return z + 1 - 2 * (z % 2)
    if k == 2:
        return z + 2 - 4 * (z // 2)
    return 3 - z


def kernel(
    lat_ref, mod_ref, wq_hbm, wo_hbm, out_ref,
    wq, wo, xh, nm, qb, kv, osend, orecv, lsend, lrecv, att, attx, gate, gatex,
    psend, precv, zsend, zrecv, fin, finx,
    w_sem, xs_sem, xr_sem, x2_sem, g_sem, qs_sem, qr_sem, q3_sem, ks_sem, kr_sem, k2_sem,
    os_sem, or_sem, ls_sem, lr_sem, as_sem, ar_sem, ps_sem, pr_sem, zs_sem, zr_sem, fs_sem, fr_sem,
):
    b, s, h = lax.axis_index("branch"), lax.axis_index("seq"), lax.axis_index("head")
    x, z, y, zh = s // NZ, s % NZ, h // 2, h % 2

    def to_y(d):
        return (b, s, ((y + d) % NY) * 2 + zh)

    def to_x(d):
        return (b, ((x + d) % NX) * NZ + z, h)

    def to_z(k):
        return (b, x * NZ + toggled(z, k), h)

    far = (b, s, h + 1 - 2 * zh)
    twin = (1 - b, s, h)
    inner = (z == 1) | (z == 2)

    def remote(src, dst, ssem, rsem, dev):
        return pltpu.make_async_remote_copy(
            src_ref=src, dst_ref=dst, send_sem=ssem, recv_sem=rsem,
            device_id=dev, device_id_type=MESH,
        )

    load_q = pltpu.make_async_copy(wq_hbm, wq, w_sem.at[0])
    load_o = pltpu.make_async_copy(wo_hbm, wo, w_sem.at[1])
    load_q.start()
    load_o.start()

    barrier = pltpu.get_barrier_semaphore()
    peers = [to_y(d) for d in YD] + [to_x(d) for d in (1, 3)] + [to_z(k) for k in ZD] + [far, twin]
    for dev in peers:
        pl.semaphore_signal(barrier, inc=1, device_id=dev, device_id_type=MESH)

    def normalise(at):
        rows = lat_ref[pl.ds(pl.multiple_of(at * ROWS, ROWS), ROWS), :]
        centred = rows - jnp.mean(rows, axis=1, keepdims=True)
        var = jnp.mean(centred * centred, axis=1, keepdims=True)
        return (centred * lax.rsqrt(var + EPS)).astype(BF16).reshape(2, PART, D)

    xh[0, :, 0, 0] = normalise(b)
    weight = jnp.where(b == 0, GUIDANCE, 1.0 - GUIDANCE).astype(F32)
    gate[...] = jnp.broadcast_to(weight * mod_ref[2], gate.shape)
    pl.semaphore_wait(barrier, len(peers))

    sends = []

    def go(copy):
        copy.start()
        sends.append(copy)
        return copy

    def x_copy(src, dst, dev):
        return go(remote(xh.at[src], xh.at[dst], xs_sem.at[dst], xr_sem.at[dst], dev))

    def modulate(dz, c, half, dy):
        rows = pl.ds(((c * 2 + half) * NY + dy) * PART, PART)

        nm[dz, rows, :] = (xh[dz, c, half, dy].astype(F32) * (1.0 + mod_ref[1]) + mod_ref[0]).astype(BF16)

    tile = 512
    x_in = {}

    def spread(dz, c):
        for d in (1, 3):
            x_in[dz, c, 0, d] = x_copy((dz, c, 0, 0), (dz, c, 0, d), to_y(d))

    def pass_on(dz, d, c):
        x_in[dz, c, 0, d].wait_recv()
        side = d // 2
        cols = pl.ds(side * WIDE, WIDE)
        x_in[dz, c, 0, 2, side] = go(
            remote(
                xh.at[dz, c, 0, d, :, cols],
                xh.at[dz, c, 0, 2, :, cols],
                x2_sem.at[0, dz, c, side],
                x2_sem.at[1, dz, c, side],
                to_y(d),
            )
        )
        x_in[dz, c, 1, d] = x_copy((dz, c, 0, d), (dz, c, 1, d), twin)
        modulate(dz, c, 0, d)

    def pass_last(dz, c):
        for side in range(2):
            x_in[dz, c, 0, 2, side].wait_recv()
        x_in[dz, c, 1, 2] = x_copy((dz, c, 0, 2), (dz, c, 1, 2), twin)
        modulate(dz, c, 0, 2)

    def from_far(c):
        x_in[1, c, 0, 0].wait_recv()
        spread(1, c)
        x_in[1, c, 1, 0] = x_copy((1, c, 0, 0), (1, c, 1, 0), twin)
        modulate(1, c, 0, 0)

    def from_twin(dz, c):
        for dy in (0, 1, 3, 2):
            if (dz, dy) != (0, 0):
                x_in[dz, c, 1, dy].wait_recv()
                modulate(dz, c, 1, dy)

    for c in range(2):
        x_in[1, c, 0, 0] = x_copy((0, c, 0, 0), (1, c, 0, 0), far)
        spread(0, c)
    gate_copy = go(remote(gate, gatex, g_sem.at[0], g_sem.at[1], twin))
    xh[0, :, 1, 0] = normalise(1 - b)
    for c in range(2):
        modulate(0, c, 0, 0)
        modulate(0, c, 1, 0)

    def piece(ref, m):
        return ref.at[0, m] if m < 2 else ref.at[1 if m == 2 else 0]

    def rows_of(m):
        return CHUNK if m < 2 else 2 * CHUNK

    def parts_of(m):
        return (m,) if m < 2 else (0, 1)

    q_scale = DH**-0.5 * LOG2E
    q_in, kv_in = {}, {}

    def project(m):
        dz = m // 2
        parts = (m,) if m < 2 else (0, 1)
        rows = slice(m * CHUNK, (m + 1) * CHUNK) if m < 2 else slice(0, 2 * CHUNK)

        def to_neighbours(i):
            return [
                remote(piece(kv.at[0, i], m), piece(kv.at[d, i], m), ks_sem.at[d, i, m], kr_sem.at[d, i, m], to_x(d))
                for d in (1, 3)
            ]

        def along_line(i):
            return [
                remote(piece(qb.at[0, i], m), piece(qb.at[k, i], m), qs_sem.at[k, i, m], qr_sem.at[k, i, m], to_z(k))
                for k in (2, 1, 3)
            ]

        def per_head(i, carry):
            got = jnp.dot(nm[dz, rows], wq[i, :, DH:], preferred_element_type=F32)
            for at, c in enumerate(parts):
                mine = got[at * CHUNK : (at + 1) * CHUNK]
                kv[0, i, dz, c, 0] = mine[:, :DH].T.astype(BF16)
                kv[0, i, dz, c, 1] = mine[:, DH:].astype(BF16)
            for copy in to_neighbours(i):
                copy.start()
            got = jnp.dot(nm[dz, rows], wq[i, :, :DH], preferred_element_type=F32) * q_scale
            for at, c in enumerate(parts):
                qb[0, i, dz, c] = got[at * CHUNK : (at + 1) * CHUNK].astype(BF16)
            across, near, between = along_line(i)
            across.start()
            near.start()
            pl.when(inner)(between.start)
            return carry

        lax.fori_loop(0, H, per_head, 0)
        for i in range(H):
            kv_in[1, i, m], kv_in[3, i, m] = to_neighbours(i)
            q_in[2, i, m], q_in[1, i, m], q_in[3, i, m] = along_line(i)
            sends.extend([kv_in[1, i, m], kv_in[3, i, m], q_in[2, i, m], q_in[1, i, m]])

    def relay_x(m, i):
        for d in (1, 3):
            kv_in[d, i, m].wait_recv()
            side = d // 2
            src, dst = (piece(kv.at[at, i], m).at[side] for at in (d, 2))
            kv_in[2, i, m, side] = go(
                remote(src, dst, k2_sem.at[0, i, m, side], k2_sem.at[1, i, m, side], to_x(d))
            )

    relays = []

    def relay_z(m, i):
        q_in[2, i, m].wait_recv()
        relay = remote(piece(qb.at[2, i], m), piece(qb.at[3, i], m), q3_sem.at[i, m], qr_sem.at[3, i, m], to_z(1))
        pl.when(inner)(relay.start)
        relays.append(relay)

    for c in range(2):
        pass_on(0, 1, c)
        pass_on(0, 3, c)
    from_far(0)
    pass_last(0, 0)
    from_twin(0, 0)
    load_q.wait()
    project(0)
    from_far(1)
    pass_last(0, 1)
    from_twin(0, 1)
    project(1)
    pass_on(1, 1, 0)
    pass_on(1, 3, 0)
    relay_x(0, 0)
    pass_on(1, 1, 1)
    pass_on(1, 3, 1)
    relay_x(0, 1)
    relay_x(0, 2)
    for i in range(H):
        relay_z(0, i)
    pass_last(1, 0)
    pass_last(1, 1)
    relay_x(1, 0)
    from_twin(1, 0)
    from_twin(1, 1)
    project(2)
    relay_x(1, 1)
    relay_x(1, 2)
    for i in range(H):
        relay_z(1, i)
    for i in range(H):
        relay_x(2, i)
        relay_z(2, i)

    def attend(ks, i, m):
        rows = rows_of(m)
        query = jnp.concatenate([piece(qb.at[k, i], m)[...].reshape(rows, DH) for k in ks], axis=0)
        blocks = [(d, dz) for d in range(NX) for dz in range(2)]
        scores = jnp.concatenate(
            [
                jnp.dot(
                    query,
                    jnp.concatenate([kv[d, i, dz, 0, 0], kv[d, i, dz, 1, 0]], axis=1),
                    preferred_element_type=F32,
                )
                for d, dz in blocks
            ],
            axis=1,
        )
        peak = jnp.max(scores, axis=1, keepdims=True)
        expo = jnp.exp2(scores - peak)
        total = jnp.sum(expo, axis=1, keepdims=True)
        probs = expo.astype(BF16)
        mixed = jnp.zeros((len(ks) * rows, DH), F32)
        for at, (d, dz) in enumerate(blocks):
            mixed += jnp.dot(
                probs[:, at * 2 * CHUNK : (at + 1) * 2 * CHUNK],
                jnp.concatenate([kv[d, i, dz, 0, 1], kv[d, i, dz, 1, 1]], axis=0),
                preferred_element_type=F32,
            )
        mixed = (mixed / total).astype(BF16)
        log = jnp.broadcast_to(peak + jnp.log2(total), mixed.shape).T[:8, :]
        for at, k in enumerate(ks):
            mine = slice(at * rows, (at + 1) * rows)
            out = piece(osend.at[k, i], m)
            out[...] = mixed[mine].reshape(out.shape)
            lsend[k, i, m, :, :rows] = log[:, mine]

    o_in = {}

    def send_back(k, i, m, slot, dev):
        at = (slot, i, m)
        lanes = pl.ds(0, rows_of(m))
        o_in[at] = [
            go(remote(piece(osend.at[k, i], m), piece(orecv.at[slot, i], m), os_sem.at[at], or_sem.at[at], dev)),
            go(remote(lsend.at[k, i, m, :, lanes], lrecv.at[slot, i, m, :, lanes], ls_sem.at[at], lr_sem.at[at], dev)),
        ]

    def merged(i, m, parts):
        rows = rows_of(m)
        logs = [log[i, m, :, :rows] for _, log in parts]
        peak = functools.reduce(jnp.maximum, logs)
        shares = [jnp.exp2(log - peak) for log in logs]
        total = functools.reduce(jnp.add, shares)
        mixed = jnp.zeros((rows, DH), F32)
        for share, (out, _) in zip(shares, parts):
            column = jnp.concatenate([share / total] * (DH // 8), axis=0).T
            mixed += column * piece(out.at[i], m)[...].reshape(rows, DH).astype(F32)
        return mixed.astype(BF16), peak + jnp.log2(total)

    def cross(i, m):
        for copy in o_in[3, i, m]:
            copy.wait_recv()
        mixed, log = merged(i, m, [(osend.at[2], lsend.at[2]), (orecv.at[3], lrecv.at[3])])
        out = piece(osend.at[4, i], m)
        out[...] = mixed.reshape(out.shape)
        lsend[4, i, m, :, : rows_of(m)] = log
        send_back(4, i, m, 2, to_z(2))

    a_in = {}

    def merge(i, m):
        for k in (1, 2):
            for copy in o_in[k, i, m]:
                copy.wait_recv()
        mixed, _ = merged(
            i, m, [(osend.at[0], lsend.at[0])] + [(orecv.at[k], lrecv.at[k]) for k in (1, 2)]
        )
        for at, c in enumerate(parts_of(m)):
            for half in range(2):
                first = at * CHUNK + half * CHUNK // 2
                att[half, i, int(m == 2), c] = mixed[first : first + CHUNK // 2]
        a_in[i, m] = go(
            remote(piece(att.at[1, i], m), piece(attx.at[i], m), as_sem.at[i, m], ar_sem.at[i, m], twin)
        )

    def outgoing(i, m):
        for k in (3, 1):
            for n in (0, 1) if m == 3 else (m,):
                q_in[k, i, n].wait_recv()
        for ks in ((3,), (1,)):
            attend(ks, i, m)
            for k in ks:
                send_back(k, i, m, k, to_z(1))

    def staying(i, m):
        for ks in ((2, 0),) if m >= 2 else ((2,), (0,)):
            attend(ks, i, m)

    p_in = {}

    def project_out(m):
        for i in range(H):
            n = 3 if m < 2 and i < H - 1 else m
            if (n, m) != (3, 1):
                a_in[i, n].wait_recv()
        rows = rows_of(m) // 2
        both = jnp.concatenate(
            [
                jnp.concatenate([piece(ref.at[i], m)[...].reshape(rows, DH) for i in range(H)], axis=1)
                for ref in (att.at[0], attx)
            ],
            axis=0,
        )
        for side in range(2):

            def some(t, carry, side=side):
                cols = pl.ds(pl.multiple_of(side * WIDE + t * tile, tile), tile)
                got = jnp.dot(both, wo[:, cols], preferred_element_type=F32)
                got = (gate[0:1, cols] * got[:rows] + gatex[0:1, cols] * got[rows:]).astype(BF16)
                for at, c in enumerate(parts_of(m)):
                    mine = got[at * CHUNK // 2 : (at + 1) * CHUNK // 2].reshape(NY, PART, tile)
                    psend[side, :, m // 2, c, :, pl.ds(pl.multiple_of(t * tile, tile), tile)] = mine
                return carry

            lax.fori_loop(0, WIDE // tile, some, 0, unroll=True)
            for d in (2, 1, 3):
                at = (m, side, d)
                p_in[at] = go(
                    remote(
                        piece(psend.at[side, d], m), piece(precv.at[side, d], m), ps_sem.at[at], pr_sem.at[at], to_y(NY - d)
                    )
                )

    def summed(m, side):
        total = piece(psend.at[side, 0], m)[...].astype(F32)
        for d in (1, 3, 2):
            p_in[m, side, d].wait_recv()
            total += piece(precv.at[side, d], m)[...].astype(F32)
        return total

    def arrived(i):
        for m in range(3):
            for side in range(2):
                kv_in[2, i, m, side].wait_recv()

    def ready():
        load_o.wait()
        gate_copy.wait_recv()

    steps = [(0, 2), (1, 2), (2, 2), (0, 3), (1, 3), (2, 0), (2, 1)]
    during = {(2, 0): [lambda: project_out(2)]}
    after = {
        (0, 3): [lambda: merge(0, 2), lambda: merge(1, 2)],
        (1, 3): [ready, lambda: merge(2, 2)],
        (2, 0): [lambda: merge(0, 3)],
        (2, 1): [lambda: merge(1, 3)],
    }
    for at, (i, m) in enumerate(steps):
        if m == 2:
            arrived(i)
        outgoing(i, m)
        if at:
            cross(*steps[at - 1])
        for task in during.get((i, m), []):
            task()
        staying(i, m)
        for task in after.get((i, m), []):
            task()
    merge(2, 0)
    cross(*steps[-1])
    project_out(0)

    z_in, f_in = [], {}
    for side in range(2):
        zsend[side] = summed(2, side).astype(BF16)
        z_in.append(go(remote(zsend.at[side], zrecv.at[side], zs_sem.at[side], zr_sem.at[side], far)))
    merge(2, 1)
    project_out(1)
    for m in range(2):
        for side in range(2):
            whole = summed(m, side)
            if m == 0:
                z_in[side].wait_recv()
            whole += zrecv[side, m].astype(F32)
            fin[m, side] = whole
            f_in[m, side] = go(
                remote(fin.at[m, side], finx.at[m, side], fs_sem.at[m, side], fr_sem.at[m, side], twin)
            )
            rows = pl.ds(pl.multiple_of(b * ROWS + m * PART, PART), PART)
            out_ref[rows, side * WIDE : (side + 1) * WIDE] = whole
    for m in range(2):
        for side in range(2):
            f_in[m, side].wait_recv()
            rows = pl.ds(pl.multiple_of((1 - b) * ROWS + m * PART, PART), PART)
            out_ref[rows, side * WIDE : (side + 1) * WIDE] = finx[m, side]

    for copy in sends:
        copy.wait_send()

    @pl.when(inner)
    def _():
        for copy in relays:
            copy.wait_send()
        for m in range(3):
            for i in range(H):
                q_in[3, i, m].wait_send()


def guided(latent, modulation, wq, wo):
    dma = pltpu.SemaphoreType.DMA
    vmem = pltpu.VMEM
    scratch = [
        vmem((H, D, 3 * DH), BF16),
        vmem((H * DH, D), BF16),
        vmem((2, 2, 2, NY, PART, D), BF16),
        vmem((2, 2 * CHUNK, D), BF16),
        vmem((NZ, H, 2, 2, CHUNK, DH), BF16),
        vmem((NX, H, 2, 2, 2, DH, CHUNK), BF16),
        vmem((NZ + 1, H, 2, 2, CHUNK, DH), BF16),
        vmem((NZ, H, 2, 2, CHUNK, DH), BF16),
        vmem((NZ + 1, H, 4, 8, 2 * CHUNK), F32),
        vmem((NZ, H, 4, 8, 2 * CHUNK), F32),
        vmem((2, H, 2, 2, CHUNK // 2, DH), BF16),
        vmem((H, 2, 2, CHUNK // 2, DH), BF16),
        vmem((8, D), F32),
        vmem((8, D), F32),
        vmem((2, NY, 2, 2, PART, WIDE), BF16),
        vmem((2, NY, 2, 2, PART, WIDE), BF16),
        vmem((2, 2, PART, WIDE), BF16),
        vmem((2, 2, PART, WIDE), BF16),
        vmem((2, 2, PART, WIDE), F32),
        vmem((2, 2, PART, WIDE), F32),
        dma((2,)),
        dma((2, 2, 2, NY)), dma((2, 2, 2, NY)), dma((2, 2, 2, 2)),
        dma((2,)),
        dma((NZ, H, 3)), dma((NZ, H, 3)), dma((H, 3)),
        dma((NX, H, 3)), dma((NX, H, 3)), dma((2, H, 3, 2)),
        dma((NZ, H, 4)), dma((NZ, H, 4)),
        dma((NZ, H, 4)), dma((NZ, H, 4)),
        dma((H, 4)), dma((H, 4)),
        dma((3, 2, NY)), dma((3, 2, NY)),
        dma((2,)), dma((2,)),
        dma((2, 2)), dma((2, 2)),
    ]
    held = pl.BlockSpec(memory_space=pltpu.VMEM)
    left = pl.BlockSpec(memory_space=pl.ANY)
    return pl.pallas_call(
        kernel,
        out_shape=jax.ShapeDtypeStruct(latent.shape, F32),
        in_specs=[held, held, left, left],
        out_specs=held,
        scratch_shapes=scratch,
        compiler_params=pltpu.CompilerParams(
            collective_id=0, has_side_effects=True, vmem_limit_bytes=60 * 1024 * 1024
        ),
    )(latent, modulation, wq, wo)


def shards(latent, modulation, w_qkv, w_out, timestep):
    wq = jnp.transpose(w_qkv, (1, 0, 2))
    wo = w_out.reshape(H * DH, D)
    change = guided(latent, jnp.transpose(modulation, (1, 0, 2)), wq, wo)
    moment = timestep[0].astype(F32)
    sigma_now = sigma_at(moment)
    step_size = sigma_at(moment + 1.0) - sigma_now
    velocity = latent + change
    return (latent + step_size * velocity, latent - sigma_now * velocity)


def solution(mesh):
    placed = (
        P(("seq", "head"), None),
        P("branch", None, None),
        P(None, "head", None),
        P("head", None, None),
        P(),
    )
    return jax.shard_map(
        shards,
        mesh=mesh,
        in_specs=placed,
        out_specs=(P(("seq", "head"), None), P(("seq", "head"), None)),
        check_vma=False,
    )
```
